32 devices in a mesh: seq: 16 (over z, y, x), mp: 2 (over core).
Axes of the slice: x: 2, y: 2, z: 4, core: 2. Of those that a mesh axis runs over, the one named last changes fastest.
Arguments:
- tokens: bfloat16 [12288, 1536], P('seq'), may hold values from -6 to 6
- starts: int32 [12288], P('seq'), may hold values from 0 to 1, as said below
- w_in: bfloat16 [1536, 3, 1536], P('seq', None, 'mp'), may hold values from -0.15625 to 0.15625
- w_out: bfloat16 [1536, 1536], P('mp', 'seq'), may hold values from -0.15625 to 0.15625
- gate_up: bfloat16 [1536, 2, 6912], P('seq', None, 'mp'), may hold values from -0.15625 to 0.15625
- w_down: bfloat16 [6912, 1536], P('mp', 'seq'), may hold values from -0.078125 to 0.078125
- gain_mix: bfloat16 [1536], P('seq'), may hold values from 0.099609375 to 1.8984375
- gain_ffn: bfloat16 [1536], P('seq'), may hold values from 0.099609375 to 1.8984375
- conv_taps: bfloat16 [3, 2, 768], P(None, 'mp', 'seq'), may hold values from -3.5 to 3.5
- cotangent: bfloat16 [12288, 1536], P('seq'), may hold values from -6 to 6
Outputs:
- out_acts: bfloat16 [12288, 1536], P('seq')
- grad_tokens: float32 [12288, 1536], P('seq')
- grad_w_in: float32 [1536, 3, 1536], P('seq', None, 'mp')
- grad_w_out: float32 [1536, 1536], P('mp', 'seq')
- grad_gate_up: float32 [1536, 2, 6912], P('seq', None, 'mp')
- grad_w_down: float32 [6912, 1536], P('mp', 'seq')
- grad_gain_mix: float32 [1536], P('seq')
- grad_gain_ffn: float32 [1536], P('seq')
- grad_conv_taps: float32 [3, 2, 768], P(None, 'mp', 'seq')
The draws below stay inside these ranges and needn't reach their ends.
Inputs may be any that keep to these rules, and one draw needn't show every extreme that they name: Token 0 always starts a sequence; further starts may fall on any token, a device's first or last token included.
All inputs are finite; a program needn't handle non-finite values.
Results may differ from the reference program's by a relative error of at most 0.011.
Values may be sent and summed in bfloat16 or wider, within the bound.
No kernel may reach another device: no remote copies, remote signals or barrier semaphores. Data moves between devices by JAX's collectives and lax.ppermute only.
A program may use at most 256 MiB of HBM per device.

```python
import jax
import jax.numpy as jnp
from jax import lax

D = 1536
FF = 6912
KCONV = 3
TOK_DEV = 768
SEQ_LEN = 4096
TOKENS = 12288
N_MP = 2


def draw_starts(key, part):
    key = jax.random.fold_in(key, 11)
    pick_key = jax.random.fold_in(key, 1)
    edge_key = jax.random.fold_in(key, 2)
    second_key = jax.random.fold_in(key, 3)
    shards = TOKENS // TOK_DEV
    picks = jax.random.randint(pick_key, (TOKENS,), 0, SEQ_LEN)
    positions = jnp.arange(TOKENS, dtype=jnp.int32)
    last_edges = jax.random.randint(edge_key, (3,), 1, shards).astype(jnp.int32) * TOK_DEV - 1
    second_edges = jax.random.randint(second_key, (1,), 0, shards).astype(jnp.int32) * TOK_DEV + 1
    edges = jnp.concatenate([last_edges, second_edges])
    at_edge = jnp.any(positions[:, None] == edges[None, :], axis=1)
    first_token = positions == 0
    return jnp.where(first_token | at_edge | (picks == 0), 1, 0).astype(jnp.int32)


def raised(result, own_key, source, target, shards_of, factor):
    def block_of(axis_at):
        return (jnp.arange(result.shape[axis_at]) // (result.shape[axis_at] // shards_of)).reshape((-1,) + (1,) * (result.ndim - 1 - axis_at))

    first = jax.random.permutation(own_key, shards_of)[block_of(target)]
    second = (block_of(target) + shards_of // 2) % shards_of
    return jnp.where((block_of(source) == first) | (block_of(source) == second), factor * result, result)


def block_scale(key, dims, pieces, least, top_value):
    def one(position, parts):
        draws = jax.random.uniform(jax.random.fold_in(jax.random.fold_in(key, 6), position), (parts,), jnp.float32, least / len(pieces), top_value / len(pieces))
        return jnp.repeat(jnp.exp(draws), dims[position] // parts).reshape((-1,) + (1,) * (len(dims) - position - 1))

    level = one(*pieces[0])
    for cut in pieces[1:]:
        level = level * one(*cut)
    return level


def centred(own_key, dims, spread, reach, cuts=(), held_as=jnp.bfloat16):
    level = block_scale(own_key, dims, cuts, -0.22, 0.18) if cuts else 1.0
    drawn = jax.random.normal(own_key, dims, jnp.float32) * spread * level
    return jnp.minimum(jnp.maximum(drawn, -reach), reach).astype(held_as)


def noise_with(rng, extent, width, reach, cuts, heavy, kind=jnp.bfloat16):
    entries = width * jax.random.normal(rng, extent, jnp.float32)
    if cuts:
        entries = entries * block_scale(rng, extent, cuts, -0.22, 0.18)
    return jnp.clip(raised(entries, jax.random.fold_in(rng, 3), *heavy), -reach, reach).astype(kind)


def setup_inputs(seed: int = 0) -> dict:
    seeds = jax.random.split(jax.random.key(seed), 11)
    tokens = noise_with(seeds[0], (TOKENS, D), 1.0, 6.0, ((0, 16),), (0, 1, 16, 2.0))
    starts = draw_starts(jax.random.fold_in(seeds[10], 71), 0)
    w_in = centred(seeds[2], (D, 3, D), D ** -0.5, 0.15625, ((0, 16), (2, 2)))
    w_out = centred(seeds[3], (D, D), D ** -0.5, 0.15625, ((0, 2), (1, 16)))
    gate_up = centred(seeds[4], (D, 2, FF), D ** -0.5, 0.15625, ((0, 16), (2, 2)))
    w_down = centred(seeds[5], (FF, D), FF ** -0.5, 0.078125, ((0, 2), (1, 16)))
    gain_mix = jnp.clip(1.0 + 0.18 * jax.random.normal(seeds[6], (D,), jnp.float32), 0.099609375, 1.8984375).astype(jnp.bfloat16)
    gain_ffn = jnp.clip(1.0 + 0.18 * jax.random.normal(seeds[7], (D,), jnp.float32), 0.099609375, 1.8984375).astype(jnp.bfloat16)
    conv_taps = centred(seeds[8], (KCONV, N_MP, D // N_MP), KCONV ** -0.5, 3.5, ((1, 2), (2, 16)))
    cotangent = noise_with(seeds[9], (TOKENS, D), 1.0, 6.0, ((0, 16),), (0, 1, 16, 2.0))
    return {"tokens": tokens, "starts": starts, "w_in": w_in, "w_out": w_out, "gate_up": gate_up, "w_down": w_down, "gain_mix": gain_mix, "gain_ffn": gain_ffn, "conv_taps": conv_taps, "cotangent": cotangent}


@jax.custom_vjp
def low(v):
    return lax.optimization_barrier(v.astype(jnp.bfloat16)).astype(jnp.float32)

@jax.custom_vjp
def low_back(v):
    return v

def low_keep(v):
    return (low(v), None)

def low_pass(kept, grad):
    return (grad,)

def back_keep(v):
    return (v, None)

def back_low(kept, grad):
    return (low(grad),)
low.defvjp(low_keep, low_pass)
low_back.defvjp(back_keep, back_low)
epsilon = 1e-05

def rms_norm(values, gain):
    return values * lax.rsqrt(lax.optimization_barrier(jnp.mean(values * values, axis=-1, keepdims=True)) + epsilon) * gain

def keep_masks(starts):
    begins = starts.astype(jnp.float32)
    earlier = jnp.concatenate([jnp.zeros((1,), jnp.float32), begins[:-1]])
    keep_one = 1.0 - begins
    keep_two = (1.0 - begins) * (1.0 - earlier)
    return (keep_one[:, None], keep_two[:, None])

def forward(tokens, w_in, w_out, gate_up, w_down, gain_mix, gain_ffn, conv_taps, keep_one, keep_two):
    highest = lax.Precision.HIGHEST
    norm_mix = low(rms_norm(tokens, gain_mix))
    projected = low_back(jnp.einsum('td,dkc->tkc', norm_mix, w_in, precision=highest))
    b_part = projected[:, 0]
    c_part = projected[:, 1]
    x_part = projected[:, 2]
    mixed_in = low_back(low(b_part * x_part))
    zero_row = jnp.zeros((1, D), jnp.float32)
    one_back = jnp.concatenate([zero_row, mixed_in[:-1]], axis=0)
    two_back = jnp.concatenate([zero_row, zero_row, mixed_in[:-2]], axis=0)
    taps = conv_taps.reshape(KCONV, D)
    convolved = taps[0] * mixed_in + taps[1] * keep_one * one_back + taps[2] * keep_two * two_back
    gated = low(c_part * convolved)
    mixer = low_back(jnp.dot(gated, w_out, precision=highest))
    middle = tokens + mixer
    norm_ffn = low(rms_norm(middle, gain_ffn))
    gate_vals = low_back(jnp.einsum('td,dkf->tkf', norm_ffn, gate_up, precision=highest))
    act_vals = low(jax.nn.silu(gate_vals[:, 0]) * gate_vals[:, 1])
    return middle + jnp.dot(act_vals, w_down, precision=highest)

def reference(tokens, starts, w_in, w_out, gate_up, w_down, gain_mix, gain_ffn, conv_taps, cotangent):
    keep_one, keep_two = keep_masks(starts)
    floats = tuple((item.astype(jnp.float32) for item in (tokens, w_in, w_out, gate_up, w_down, gain_mix, gain_ffn, conv_taps)))

    def run_block(tok_vals, win_vals, wout_vals, gu_vals, down_vals, gmix_vals, gffn_vals, taps_vals):
        return forward(tok_vals, win_vals, wout_vals, gu_vals, down_vals, gmix_vals, gffn_vals, taps_vals, keep_one, keep_two)
    output, pullback = jax.vjp(run_block, *floats)
    grads = pullback(cotangent.astype(jnp.float32))
    return (output.astype(jnp.bfloat16), grads[0], grads[1], grads[2], grads[3], grads[4], grads[5], grads[6], grads[7])
```

```python
import jax
import jax.numpy as jnp
import numpy as np
from jax import lax
from jax.sharding import Mesh, PartitionSpec as P

epsilon = 1e-05
f32 = jnp.float32
bf16 = jnp.bfloat16
PLANE = ("y", "x")
SWAP = ((0, 1), (1, 0))


def dot(left, right, dims):
    return lax.dot_general(left, right, ((dims[0], dims[1]), ((), ())), preferred_element_type=f32)


def by_xor(stack):
    x_bit, y_bit = lax.axis_index("x") == 1, lax.axis_index("y") == 1
    stack = jnp.where(x_bit, jnp.stack([stack[1], stack[0], stack[3], stack[2]]), stack)
    return jnp.where(y_bit, jnp.stack([stack[2], stack[3], stack[0], stack[1]]), stack)


def plane_swap(value, offset):
    if offset == 1:
        return lax.ppermute(value, "x", SWAP)
    if offset == 2:
        return lax.ppermute(value, "y", SWAP)
    return lax.ppermute(value, PLANE, [(i, i ^ 3) for i in range(4)])


def plane_exchange(stack):
    relative = by_xor(stack)
    got = [relative[0]] + [plane_swap(relative[r], r) for r in (1, 2, 3)]
    return by_xor(jnp.stack(got))


def plane_gather(own):
    half = own.shape[0] // 32 * 16
    from_x = plane_swap(own, 1)
    from_y = plane_swap(own, 2)
    top = plane_swap(from_x[:half], 2)
    low = plane_swap(from_y[half:], 1)
    return [own, from_x, from_y, jnp.concatenate([top, low], axis=0)]


def plane_reduce(parts):
    half = parts.shape[1] // 32 * 16
    low_in = plane_swap(jnp.stack([parts[1, half:], parts[3, half:]]), 1)
    top_in = plane_swap(jnp.stack([parts[2, :half], parts[3, :half]]), 2)
    low_on = (parts[2, half:].astype(f32) + low_in[1].astype(f32)).astype(bf16)
    top_on = (parts[1, :half].astype(f32) + top_in[1].astype(f32)).astype(bf16)
    low_last = plane_swap(low_on, 2)
    top_last = plane_swap(top_on, 1)
    top = parts[0, :half].astype(f32) + top_in[0].astype(f32) + top_last.astype(f32)
    low = parts[0, half:].astype(f32) + low_in[0].astype(f32) + low_last.astype(f32)
    return jnp.concatenate([top, low], axis=0)


def core_swap(value):
    return lax.ppermute(value, "mp", SWAP)


def halves_turned(value):
    width = value.shape[-1] // 2
    return jnp.concatenate([value[..., width:], value[..., :width]], axis=-1)


def halo_forward(tails):
    planes = lax.axis_size("z")
    tails = halves_turned(tails)
    got = core_swap(tails)
    jump = [(2 * z + 1, 2 * z + 2) for z in range(planes - 1)]
    before = lax.ppermute(by_xor(tails)[3], ("z", "mp"), jump)
    shifted = by_xor(jnp.concatenate([before[None], by_xor(got)[:3]], axis=0))
    return jnp.where(lax.axis_index("mp") == 1, got, shifted)


def halo_backward(heads):
    planes = lax.axis_size("z")
    heads = halves_turned(heads)
    got = core_swap(heads)
    jump = [(2 * z + 2, 2 * z + 1) for z in range(planes - 1)]
    after = lax.ppermute(by_xor(heads)[0], ("z", "mp"), jump)
    shifted = by_xor(jnp.concatenate([by_xor(got)[1:], after[None]], axis=0))
    return jnp.where(lax.axis_index("mp") == 1, shifted, got)


def both_cores(own):
    other = core_swap(own)
    first = lax.axis_index("mp") == 0
    return jnp.concatenate([jnp.where(first, own, other), jnp.where(first, other, own)], axis=0)


def per_device(
    tokens, starts, w_in, w_out, gate_up, w_down, gain_mix, gain_ffn, conv_taps, cotangent
):
    planes = lax.axis_size("z")
    core = lax.axis_index("mp")
    rows, _, half_c = w_in.shape
    half_f = w_down.shape[0]
    width = tokens.shape[1]
    seg = tokens.shape[0] // 2
    chan, hid = half_c // 4, half_f // 4
    pad = -hid % 128
    hid_p = hid + pad
    plane_rows = 4 * rows
    tap_len = conv_taps.shape[2]

    def mine(value):
        return lax.dynamic_slice_in_dim(value, core * seg, seg, axis=0)

    gain_one = gain_mix.astype(f32)[:, None, None]
    gain_two = gain_ffn.astype(f32)[:, None, None]
    in_scaled = (w_in.astype(f32) * gain_one).astype(bf16).reshape(rows, 3, 4, chan)
    in_quart = jnp.transpose(in_scaled, (2, 0, 1, 3)).reshape(4, rows, 3 * chan)
    out_quart = jnp.transpose(w_out.reshape(4, chan, rows), (0, 2, 1))
    conv_pack = plane_exchange(jnp.concatenate([in_quart, out_quart], axis=2))
    conv_pack = conv_pack.reshape(plane_rows, 4 * chan)
    tap_piece = lax.ppermute(
        conv_taps.reshape(1, 3 * tap_len),
        ("z",) + PLANE,
        [(s, (s % planes) * 4 + s // planes) for s in range(4 * planes)],
    )
    tap_rows = jnp.pad(tap_piece, ((0, 15), (0, 4 * chan - 3 * tap_len)))
    conv_pack = jnp.concatenate([conv_pack, tap_rows], axis=0)
    conv_own = lax.all_gather(conv_pack, "z", axis=0, tiled=False)

    down_quart = jnp.transpose(w_down.reshape(4, hid, rows), (0, 2, 1))
    down_quart = jnp.pad(down_quart, ((0, 0), (0, 0), (0, pad)))
    down_pack = plane_exchange(down_quart).reshape(plane_rows, hid_p)
    down_own = lax.all_gather(down_pack, "z", axis=0, tiled=True)

    gu_scaled = (gate_up.astype(f32) * gain_two).astype(bf16).reshape(rows, 2, 4, hid)
    gu_quart = jnp.pad(jnp.transpose(gu_scaled, (2, 0, 1, 3)), ((0, 0),) * 3 + ((0, pad),))
    gu_pack = plane_exchange(gu_quart.reshape(4, rows, 2 * hid_p)).reshape(plane_rows, 2 * hid_p)
    gu_own = lax.all_gather(gu_pack, "z", axis=0, tiled=True)

    inputs = mine(tokens).astype(f32)
    inv_mix = lax.rsqrt(jnp.mean(inputs * inputs, axis=-1, keepdims=True) + epsilon)
    hat_mix = inputs * inv_mix
    begin_row = mine(starts).astype(bf16)[None]
    begin_rows = jnp.pad(begin_row, ((0, 15), (0, width - seg)))
    hat_all = plane_gather(jnp.concatenate([hat_mix.astype(bf16), begin_rows], axis=0))
    begins = jnp.stack([blk[seg, :seg] for blk in hat_all]).astype(f32)
    hat_all = jnp.concatenate([blk[:seg] for blk in hat_all], axis=0)
    cot = mine(cotangent)
    cot_all = jnp.concatenate(plane_gather(cot), axis=0)

    earlier = jnp.concatenate([jnp.zeros((4, 1), f32), begins[:, :-1]], axis=1)
    keep_one = (1.0 - begins)[:, :, None]
    keep_two = ((1.0 - begins) * (1.0 - earlier))[:, :, None]
    last_keep = 1.0 - begins[:, -1:]

    conv_other = core_swap(conv_own)
    pair = [conv_own, conv_other]
    taps = jnp.concatenate(
        [
            jnp.transpose(
                p[:, plane_rows, : 3 * tap_len].reshape(planes, 3, tap_len), (1, 0, 2)
            ).reshape(3, chan)
            for p in pair
        ],
        axis=1,
    ).astype(f32)
    in_full = jnp.concatenate(
        [p[:, :plane_rows, : 3 * chan].reshape(width, 3, chan) for p in pair], axis=2
    ).reshape(width, 6 * chan)
    out_full = jnp.concatenate(
        [p[:, :plane_rows, 3 * chan :].reshape(width, chan) for p in pair], axis=1
    )
    projected = dot(hat_all, in_full, ((1,), (0,))).reshape(4, seg, 6 * chan)
    b_part = projected[:, :, : 2 * chan]
    c_part = projected[:, :, 2 * chan : 4 * chan]
    x_part = projected[:, :, 4 * chan :]
    mixed_in = (b_part * x_part).astype(bf16)
    tails = jnp.stack(
        [(mixed_in[:, -2] * last_keep).astype(bf16), mixed_in[:, -1]], axis=1
    )
    extended = jnp.concatenate([halo_forward(tails), mixed_in], axis=1).astype(f32)
    convolved = (
        taps[0] * extended[:, 2:]
        + taps[1] * keep_one * extended[:, 1:-1]
        + taps[2] * keep_two * extended[:, :-2]
    )
    gated = (c_part * convolved).astype(bf16).reshape(4 * seg, 2 * chan)
    mixer = dot(gated, out_full, ((1,), (1,))).astype(bf16).reshape(4, seg, width)
    middle = inputs + plane_reduce(mixer)

    inv_ffn = lax.rsqrt(jnp.mean(middle * middle, axis=-1, keepdims=True) + epsilon)
    hat_ffn = middle * inv_ffn
    hat2_all = jnp.concatenate(plane_gather(hat_ffn.astype(bf16)), axis=0)
    down_other = core_swap(down_own)
    gu_other = core_swap(gu_own)
    acts, grads = [], []
    for down, gu in ((down_own, gu_own), (down_other, gu_other)):
        grad_act = dot(cot_all, down, ((1,), (0,)))
        gate_vals = dot(hat2_all, gu, ((1,), (0,)))
        gate_part, up_part = gate_vals[:, :hid_p], gate_vals[:, hid_p:]
        sig_gate = jax.nn.sigmoid(gate_part)
        silu_gate = gate_part * sig_gate
        acts.append((silu_gate * up_part).astype(bf16))
        grad_gate = grad_act * up_part * sig_gate * (1.0 + gate_part * (1.0 - sig_gate))
        grads.append(jnp.concatenate([grad_gate, grad_act * silu_gate], axis=1).astype(bf16))
    grad_hat2 = (dot(grads[0], gu_own, ((1,), (1,))) + dot(grads[1], gu_other, ((1,), (1,)))).astype(bf16)
    ffn_out = (dot(acts[0], down_own, ((1,), (1,))) + dot(acts[1], down_other, ((1,), (1,)))).astype(bf16)

    def weight_grad(left, own_right, other_right):
        theirs = core_swap(dot(left, other_right, ((0,), (0,))).astype(bf16))
        return (dot(left, own_right, ((0,), (0,))) + theirs.astype(f32)).astype(bf16)

    grad_down = weight_grad(cot_all, acts[0], acts[1])
    grad_down = lax.psum_scatter(grad_down, "z", scatter_dimension=0, tiled=True)
    grad_gu = weight_grad(hat2_all, grads[0], grads[1])
    grad_gu = lax.psum_scatter(grad_gu, "z", scatter_dimension=0, tiled=True)

    grad_hat2 = plane_reduce(grad_hat2.reshape(4, seg, width))
    inner = jnp.mean(grad_hat2 * hat_ffn, axis=-1, keepdims=True)
    grad_middle = cot.astype(f32) + inv_ffn * (grad_hat2 - hat_ffn * inner)
    output_vals = (middle + plane_reduce(ffn_out.reshape(4, seg, width))).astype(bf16)

    grad_mixer = jnp.concatenate(plane_gather(grad_middle.astype(bf16)), axis=0)
    grad_gated = dot(grad_mixer, out_full, ((1,), (0,))).reshape(4, seg, 2 * chan)
    grad_out = dot(grad_mixer, gated, ((0,), (0,)))
    grad_c = grad_gated * convolved
    grad_conv = grad_gated * c_part
    grad_taps = jnp.stack(
        [
            jnp.sum(grad_conv * extended[:, 2:], axis=(0, 1)),
            jnp.sum(grad_conv * keep_one * extended[:, 1:-1], axis=(0, 1)),
            jnp.sum(grad_conv * keep_two * extended[:, :-2], axis=(0, 1)),
        ]
    )
    term_zero = taps[0] * grad_conv
    term_one = taps[1] * keep_one * grad_conv
    term_two = taps[2] * keep_two * grad_conv
    grad_ext = (
        jnp.pad(term_zero, ((0, 0), (2, 0), (0, 0)))
        + jnp.pad(term_one, ((0, 0), (1, 1), (0, 0)))
        + jnp.pad(term_two, ((0, 0), (0, 2), (0, 0)))
    )
    back = halo_backward(grad_ext[:, :2])
    tail_gate = jnp.stack([last_keep, jnp.ones((4, 1), f32)], axis=1)
    grad_mixed = jnp.concatenate(
        [grad_ext[:, 2:-2], grad_ext[:, -2:] + back * tail_gate], axis=1
    )
    grad_mixed = grad_mixed.astype(bf16).astype(f32)
    grad_proj = jnp.concatenate(
        [grad_mixed * x_part, grad_c, grad_mixed * b_part], axis=2
    ).astype(bf16).reshape(4 * seg, 6 * chan)
    grad_hat1 = dot(grad_proj, in_full, ((1,), (1,))).astype(bf16)
    grad_in = dot(hat_all, grad_proj, ((0,), (0,))).reshape(width, 3, 2, chan)

    def conv_half(which):
        body = jnp.concatenate(
            [
                grad_in[:, :, which].reshape(width, 3 * chan),
                grad_out[:, which * chan : (which + 1) * chan],
            ],
            axis=1,
        ).reshape(planes, plane_rows, 4 * chan)
        piece = grad_taps[:, which * chan : (which + 1) * chan].reshape(3, planes, tap_len)
        piece = jnp.transpose(piece, (1, 0, 2)).reshape(planes, 1, 3 * tap_len)
        piece = jnp.pad(piece, ((0, 0), (0, 15), (0, 4 * chan - 3 * tap_len)))
        return jnp.concatenate([body, piece], axis=1)

    theirs = core_swap(conv_half(1).astype(bf16))
    conv_grads = (conv_half(0) + theirs.astype(f32)).astype(bf16)
    conv_grads = lax.psum_scatter(conv_grads, "z", scatter_dimension=0, tiled=False)

    grad_hat1 = plane_reduce(grad_hat1.reshape(4, seg, width))
    inner = jnp.mean(grad_hat1 * hat_mix, axis=-1, keepdims=True)
    grad_inputs = grad_middle + inv_mix * (grad_hat1 - hat_mix * inner)

    red_down = plane_exchange(grad_down.reshape(4, rows, hid_p))[:, :, :hid]
    red_down = jnp.transpose(red_down, (0, 2, 1)).reshape(half_f, rows).astype(f32)
    red_gu = plane_exchange(grad_gu.reshape(4, rows, 2 * hid_p)).reshape(4, rows, 2, hid_p)
    red_gu = jnp.transpose(red_gu[..., :hid], (1, 2, 0, 3)).reshape(rows, 2, half_f).astype(f32)
    red_conv = plane_exchange(conv_grads[:plane_rows].reshape(4, rows, 4 * chan)).astype(f32)
    red_in = red_conv[:, :, : 3 * chan].reshape(4, rows, 3, chan)
    red_in = jnp.transpose(red_in, (1, 2, 0, 3)).reshape(rows, 3, half_c)
    red_out = jnp.transpose(red_conv[:, :, 3 * chan :], (0, 2, 1)).reshape(half_c, rows)
    red_taps = lax.ppermute(
        conv_grads[plane_rows, : 3 * tap_len].astype(f32).reshape(3, 1, tap_len),
        ("z",) + PLANE,
        [((s % planes) * 4 + s // planes, s) for s in range(4 * planes)],
    )
    gains = jnp.stack(
        [
            jnp.sum(red_in * w_in.astype(f32), axis=(1, 2)),
            jnp.sum(red_gu * gate_up.astype(f32), axis=(1, 2)),
        ]
    )
    gains = gains + core_swap(gains)
    return (
        both_cores(output_vals),
        both_cores(grad_inputs),
        red_in * gain_one,
        red_out,
        red_gu * gain_two,
        red_down,
        gains[0],
        gains[1],
        red_taps,
    )


def solution(mesh):
    seq, cores = mesh.shape["seq"], mesh.shape["mp"]
    split = Mesh(np.asarray(mesh.devices).reshape(seq // 4, 2, 2, cores), ("z", "y", "x", "mp"))
    by = ("z", "y", "x")
    weights = (
        P(by, None, "mp"),
        P("mp", by),
        P(by, None, "mp"),
        P("mp", by),
        P(by),
        P(by),
        P(None, "mp", by),
    )
    return jax.shard_map(
        per_device,
        mesh=split,
        in_specs=(P(by, None), P(by)) + weights + (P(by, None),),
        out_specs=(P(by, None), P(by, None)) + weights,
        check_vma=False,
    )
```

```python
import functools

import jax
import jax.numpy as jnp
import numpy as np
from jax import lax
from jax.experimental import pallas as pl
from jax.experimental.pallas import tpu as pltpu
from jax.sharding import Mesh, PartitionSpec as P

epsilon = 1e-05
f32 = jnp.float32
bf16 = jnp.bfloat16
PLANE = ("y", "x")
SWAP = ((0, 1), (1, 0))
LANES = 128
VMEM_LIMIT = 50 * 1024 * 1024


def nn(left, right):
    return lax.dot_general(left, right, (((1,), (0,)), ((), ())), preferred_element_type=f32)


def nt(left, right):
    return lax.dot_general(left, right, (((1,), (1,)), ((), ())), preferred_element_type=f32)


def tn(left, right):
    return lax.dot_general(left, right, (((0,), (0,)), ((), ())), preferred_element_type=f32)


def after(value, *others):
    return lax.optimization_barrier((value,) + others)[0]


def by_xor(stack, bits):
    places = np.arange(stack.shape[0])
    for level, bit in enumerate(bits):
        turned = jnp.stack([stack[int(p)] for p in places ^ (1 << level)])
        stack = jnp.where(bit, turned, stack)
    return stack


def plane_bits():
    return [lax.axis_index("x") == 1, lax.axis_index("y") == 1]


def plane_swap(value, offset):
    if offset == 1:
        return lax.ppermute(value, "x", SWAP)
    if offset == 2:
        return lax.ppermute(value, "y", SWAP)
    return lax.ppermute(value, PLANE, [(i, i ^ 3) for i in range(4)])


def core_swap(value):
    return lax.ppermute(value, "mp", SWAP)


def exchange_first(relative):
    return [relative[0]] + [plane_swap(relative[r], r) for r in (1, 2, 3)]


def exchange_second(got):
    return by_xor(jnp.stack(got), plane_bits())


def plane_exchange(stack):
    return exchange_second(exchange_first(by_xor(stack, plane_bits())))


def gather_first(own):
    return plane_swap(own, 1), plane_swap(own, 2)


def gather_second(own, from_x, from_y):
    half = own.shape[0] // 32 * 16
    return [own, from_x, from_y, plane_swap(from_x[:half], 2), plane_swap(from_y[half:], 1)]


def plane_gather(own):
    return gather_second(own, *gather_first(own))


def reduce_first(parts):
    to_x, to_y = parts[0], parts[1]
    return plane_swap(to_x, 1), plane_swap(to_y, 2)


def reduce_second(parts, low_in, top_in):
    _, _, _, mine_x, mine_y = parts
    top_on = (mine_x.astype(f32) + top_in[1].astype(f32)).astype(bf16)
    low_on = (mine_y.astype(f32) + low_in[1].astype(f32)).astype(bf16)
    return plane_swap(top_on, 1), plane_swap(low_on, 2)


def reduce_end(parts, low_in, top_in, top_last, low_last):
    own = parts[2].astype(f32)
    half = top_last.shape[0]
    top = own[:half] + top_in[0].astype(f32) + top_last.astype(f32)
    low = own[half:] + low_in[0].astype(f32) + low_last.astype(f32)
    return jnp.concatenate([top, low], axis=0)


def plane_reduce(parts, *held):
    low_in, top_in = reduce_first(parts)
    top_last, low_last = reduce_second(parts, low_in, top_in)
    if held:
        top_last, low_last = lax.optimization_barrier((top_last, low_last) + held)[:2]
    return reduce_end(parts, low_in, top_in, top_last, low_last)


def halo_forward(tails):
    planes = lax.axis_size("z")
    got = core_swap(tails)
    jump = [(2 * z + 1, 2 * z + 2) for z in range(planes - 1)]
    ordered = by_xor(jnp.moveaxis(tails, 1, 0), plane_bits())
    before = lax.ppermute(ordered[3], ("z", "mp"), jump)
    ordered = by_xor(jnp.moveaxis(got, 1, 0), plane_bits())
    shifted = by_xor(jnp.concatenate([before[None], ordered[:3]], axis=0), plane_bits())
    return jnp.where(lax.axis_index("mp") == 1, got, jnp.moveaxis(shifted, 0, 1))


def halo_backward(heads):
    planes = lax.axis_size("z")
    got = core_swap(heads)
    jump = [(2 * z + 2, 2 * z + 1) for z in range(planes - 1)]
    ordered = by_xor(jnp.moveaxis(heads, 1, 0), plane_bits())
    behind = lax.ppermute(ordered[0], ("z", "mp"), jump)
    ordered = by_xor(jnp.moveaxis(got, 1, 0), plane_bits())
    shifted = by_xor(jnp.concatenate([ordered[1:], behind[None]], axis=0), plane_bits())
    return jnp.where(lax.axis_index("mp") == 1, jnp.moveaxis(shifted, 0, 1), got)


def both_cores(own):
    other = core_swap(own)
    first = lax.axis_index("mp") == 0
    return jnp.concatenate([jnp.where(first, own, other), jnp.where(first, other, own)], axis=0)


def taps_turn(back):
    planes = lax.axis_size("z")
    pairs = [(s, (s % planes) * 4 + s // planes) for s in range(4 * planes)]
    return [(b, a) for a, b in pairs] if back else pairs


def call(body, out_shapes, *args, grid=None, in_specs=None, out_specs=None, prefetch=0, flops=0, aliases=None):
    whole = pl.BlockSpec(memory_space=pltpu.VMEM)
    if in_specs is None:
        in_specs = [whole] * (len(args) - prefetch)
    if out_specs is None:
        out_specs = [whole] * len(out_shapes)
    moved = sum(a.size * a.dtype.itemsize for a in args)
    moved += sum(o.size * o.dtype.itemsize for o in out_shapes)
    return pl.pallas_call(
        body,
        out_shape=out_shapes,
        grid_spec=pltpu.PrefetchScalarGridSpec(
            num_scalar_prefetch=prefetch,
            grid=grid or (),
            in_specs=in_specs,
            out_specs=out_specs,
        ),
        input_output_aliases=aliases or {},
        compiler_params=pltpu.CompilerParams(vmem_limit_bytes=VMEM_LIMIT),
        cost_estimate=pl.CostEstimate(flops=flops // 1000, bytes_accessed=moved // 1000, transcendentals=0),
    )(*args)


def out(shape, dtype):
    return jax.ShapeDtypeStruct(shape, dtype)


def spans(seg):
    half = seg // 2
    return ((0, 0, 0, seg), (1, 1, 0, seg), (2, 2, 0, seg), (3, 3, 0, half), (4, 3, half, seg - half))


def split_shapes(seg, width):
    half = seg // 2
    return [
        out((2, half, width), bf16),
        out((2, half, width), bf16),
        out((seg, width), bf16),
        out((half, width), bf16),
        out((half, width), bf16),
    ]


def split_store(refs, place, value):
    to_x, to_y, own, mine_x, mine_y = refs
    value = value.astype(bf16)
    half = value.shape[0] // 2
    top, low = value[:half], value[half:]
    if place == 0:
        own[...] = value
    elif place == 1:
        mine_x[...] = top
        to_x[0] = low
    elif place == 2:
        to_y[0] = top
        mine_y[...] = low
    else:
        to_y[1] = top
        to_x[1] = low


def conv_project(hats, pack, seg):
    planes, _, rows_taps, cols = pack.shape
    rows, chan = rows_taps - 16, cols // 4
    width = planes * rows

    def body(*refs):
        hat_refs, pack_ref, b_ref, c_ref, x_ref, u_ref = refs[:5], *refs[5:]
        for half in range(2):
            weights = pack_ref[:, half, :rows, :].reshape(width, cols)
            for place, segment, low, count in spans(seg):
                proj = nn(hat_refs[place][:count, :], weights)
                b_val, c_val, x_val = (
                    proj[:, :chan],
                    proj[:, chan : 2 * chan],
                    proj[:, 3 * chan :],
                )
                at = (half, segment, pl.ds(low, count))
                b_ref[at] = b_val
                c_ref[at] = c_val
                x_ref[at] = x_val
                u_ref[at] = (b_val * x_val).astype(bf16)

    shape = (2, 4, seg, chan)
    return call(
        body,
        [out(shape, f32)] * 3 + [out(shape, bf16)],
        *hats,
        pack,
        flops=2 * 4 * seg * width * cols * 2,
    )


def rows_of(shape):
    return lax.broadcasted_iota(jnp.int32, shape, 0)


def earlier_rows(value, halo):
    row = rows_of(value.shape)
    one = jnp.where(row == 0, halo[1:2], pltpu.roll(value, 1, 0))
    two = jnp.where(row == 0, halo[0:1], jnp.where(row == 1, halo[1:2], pltpu.roll(value, 2, 0)))
    return one, two


def conv_mix(u_vals, halo, c_part, keeps, taps, pack, seg):
    planes, _, rows_taps, cols = pack.shape
    rows, chan = rows_taps - 16, cols // 4
    width = planes * rows

    def body(u_ref, halo_ref, c_ref, keep_ref, taps_ref, pack_ref, v_ref, y_ref, *split):
        outs = [
            pack_ref[:, half, :rows, 2 * chan : 3 * chan].reshape(width, chan) for half in range(2)
        ]
        for segment in range(4):
            keep_one, keep_two = keep_ref[0, segment], keep_ref[1, segment]
            total = None
            for half in range(2):
                u_val = u_ref[half, segment].astype(f32)
                one, two = earlier_rows(u_val, halo_ref[half, segment])
                tap = taps_ref[half]
                v_val = tap[0:1] * u_val + tap[1:2] * keep_one * one + tap[2:3] * keep_two * two
                y_val = (c_ref[half, segment] * v_val).astype(bf16)
                v_ref[half, segment] = v_val
                y_ref[half, segment] = y_val
                term = nt(y_val, outs[half])
                total = term if total is None else total + term
            split_store(split, segment, total)

    shape = (2, 4, seg, chan)
    results = call(
        body,
        [out(shape, f32), out(shape, bf16)] + split_shapes(seg, width),
        u_vals,
        halo,
        c_part,
        keeps,
        taps,
        pack,
        flops=2 * 4 * seg * width * 2 * chan,
    )
    return results[0], results[1], results[2:]


def conv_back(grad_mixer, u_vals, halo, c_part, v_vals, keeps, taps, pack, seg):
    planes, _, rows_taps, cols = pack.shape
    rows, chan = rows_taps - 16, cols // 4
    width = planes * rows

    def body(*refs):
        mix_refs = refs[:5]
        u_ref, halo_ref, c_ref, v_ref, keep_ref, taps_ref, pack_ref = refs[5:12]
        dc_ref, dv_ref, sums_ref, heads_ref = refs[12:]
        for half in range(2):
            outs = pack_ref[:, half, :rows, 2 * chan : 3 * chan].reshape(width, chan)
            for place, segment, low, count in spans(seg):
                at = (half, segment, pl.ds(low, count))
                grad_y = nn(mix_refs[place][:count, :], outs)
                dc_ref[at] = (grad_y * v_ref[at]).astype(bf16)
                dv_ref[at] = grad_y * c_ref[at]
            sums = [jnp.zeros((1, chan), f32)] * 3
            tap = taps_ref[half]
            for segment in range(4):
                keep_one, keep_two = keep_ref[0, segment], keep_ref[1, segment]
                u_val = u_ref[half, segment].astype(f32)
                one, two = earlier_rows(u_val, halo_ref[half, segment])
                grad_v = dv_ref[half, segment]
                once, twice = keep_one * grad_v, keep_two * grad_v
                for k, term in enumerate((grad_v * u_val, once * one, twice * two)):
                    sums[k] = sums[k] + jnp.sum(term, axis=0, keepdims=True)
                heads_ref[half, segment, 0:1] = tap[2:3] * twice[0:1]
                heads_ref[half, segment, 1:2] = tap[1:2] * once[0:1] + tap[2:3] * twice[1:2]
            for k in range(3):
                sums_ref[half, k : k + 1] = sums[k]

    shape = (2, 4, seg, chan)
    return call(
        body,
        [out(shape, bf16), out(shape, f32), out((2, 3, chan), f32), out((2, 4, 2, chan), f32)],
        *grad_mixer,
        u_vals,
        halo,
        c_part,
        v_vals,
        keeps,
        taps,
        pack,
        flops=2 * 4 * seg * width * 2 * chan,
    )


def conv_grads(grad_c, grad_v, back, b_part, x_part, keeps, taps, seg):
    chan = grad_v.shape[-1]

    def body(dc_ref, dv_ref, back_ref, b_ref, x_ref, keep_ref, taps_ref, dp_ref):
        row = rows_of((seg, chan))
        for segment in range(4):
            keep_one, keep_two = keep_ref[0, segment], keep_ref[1, segment]
            for half in range(2):
                tap = taps_ref[half]
                grad_val = dv_ref[half, segment]
                once = jnp.where(row == seg - 1, 0.0, pltpu.roll(keep_one * grad_val, seg - 1, 0))
                twice = jnp.where(row >= seg - 2, 0.0, pltpu.roll(keep_two * grad_val, seg - 2, 0))
                grad_u = tap[0:1] * grad_val + tap[1:2] * once + tap[2:3] * twice
                ends = back_ref[half, segment]
                grad_u = grad_u + jnp.where(
                    row == seg - 2, ends[0:1], jnp.where(row == seg - 1, ends[1:2], 0.0)
                )
                grad_u = grad_u.astype(bf16).astype(f32)
                dp_ref[half, segment * seg : (segment + 1) * seg, :] = jnp.concatenate(
                    [
                        grad_u * x_ref[half, segment],
                        dc_ref[half, segment].astype(f32),
                        jnp.zeros((seg, chan), f32),
                        grad_u * b_ref[half, segment],
                    ],
                    axis=1,
                ).astype(bf16)

    return call(
        body,
        [out((2, 4 * seg, 4 * chan), bf16)],
        grad_c,
        grad_v,
        back,
        b_part,
        x_part,
        keeps,
        taps,
    )[0]


def ffn_pack(gate, up, down, gain, place, cuts, chan_hid):
    rows = gate.shape[0]
    hid = chan_hid

    def body(place_ref, gate_ref, up_ref, down_ref, gain_ref, *outs):
        scale = gain_ref[...]
        for q in range(4):
            for (low, high), out_ref in zip(cuts, outs):
                tiles = high - low
                for t in range(tiles):
                    start = (low + t) * LANES
                    count = min(hid - start, LANES)
                    values = [
                        ref[:, q * hid + start : q * hid + start + count]
                        for ref in (gate_ref, up_ref, down_ref)
                    ]
                    values[0] = (values[0].astype(f32) * scale).astype(bf16)
                    values[1] = (values[1].astype(f32) * scale).astype(bf16)
                    if count < LANES:
                        fill = jnp.zeros((rows, LANES - count), bf16)
                        values = [jnp.concatenate([v, fill], axis=1) for v in values]
                    for value, column in zip(values, (2 * t, 2 * t + 1, 2 * tiles + t)):
                        out_ref[q ^ place_ref[0], :, column * LANES : (column + 1) * LANES] = value

    whole = pl.BlockSpec(memory_space=pltpu.VMEM)
    return call(
        body,
        [out((4, rows, 3 * LANES * (high - low)), bf16) for low, high in cuts],
        place,
        gate,
        up,
        down,
        gain,
        in_specs=[whole] * 4,
        out_specs=[whole] * 2,
        prefetch=1,
    )


def ffn_pass(hats, cots, pack, size, seg, segments, earlier=None):
    planes, _, rows, _ = pack.shape
    width = planes * rows
    tiles = size // LANES
    blocks = [span for span in spans(seg) if span[1] in segments]
    hats, cots = ([values[span[0]] for span in blocks] for values in (hats, cots))
    count_in = len(blocks)
    first = blocks[0][1]
    held_rows = len(segments) * seg

    def body(*refs):
        hat_refs, cot_refs = refs[:count_in], refs[count_in : 2 * count_in]
        gu_ref, down_ref = refs[2 * count_in : 2 * count_in + 2]
        a_ref, dg_ref = refs[-2:]
        downs = jnp.concatenate(
            [down_ref[:, half].reshape(width, LANES) for half in range(2)], axis=1
        )
        gus = [gu_ref[:, half].reshape(width, 2 * LANES) for half in range(2)]
        for hat_ref, cot_ref, (_, segment, low, count) in zip(hat_refs, cot_refs, blocks):
            at = pl.ds((segment - first) * seg + low, count)
            grad_act = nn(cot_ref[:count, :], downs)
            for half in range(2):
                vals = nn(hat_ref[:count, :], gus[half])
                gate, up = vals[:, :LANES], vals[:, LANES:]
                grad = grad_act[:, half * LANES : (half + 1) * LANES]
                sig = 1.0 / (1.0 + jnp.exp(-gate))
                silu = gate * sig
                a_ref[half, at, :] = (silu * up).astype(bf16)
                dg_ref[half, at, :LANES] = (grad * up * (sig + silu * (1.0 - sig))).astype(bf16)
                dg_ref[half, at, LANES:] = (grad * silu).astype(bf16)

    def held(value):
        return pl.BlockSpec(value.shape, lambda t: (0, 0))

    tokens = 4 * seg
    place = first * seg // held_rows
    args = [*hats, *cots, pack, pack]
    specs = [held(v) for v in (*hats, *cots)] + [
        pl.BlockSpec((planes, 2, rows, 2 * LANES), lambda t: (0, 0, 0, t)),
        pl.BlockSpec((planes, 2, rows, LANES), lambda t: (0, 0, 0, 2 * tiles + t)),
    ]
    aliases = None
    if earlier is not None:
        aliases = {len(args): 0, len(args) + 1: 1}
        args += list(earlier)
        specs += [pl.BlockSpec(memory_space=pl.ANY)] * 2
    return call(
        body,
        [out((2, tokens, size), bf16), out((2, tokens, 2 * size), bf16)],
        *args,
        grid=(tiles,),
        in_specs=specs,
        out_specs=[
            pl.BlockSpec((2, held_rows, LANES), lambda t: (0, place, t)),
            pl.BlockSpec((2, held_rows, 2 * LANES), lambda t: (0, place, t)),
        ],
        flops=2 * held_rows * width * 6 * size,
        aliases=aliases,
    )


def turned_back(lefts, packs, place, rows, seg):
    planes = packs[0].shape[0]
    width = planes * rows
    group = max(1, 2 * planes // 4)
    wide = group * rows

    def body(*refs):
        count = len(lefts)
        left_refs, pack_refs, split = refs[:count], refs[count : 2 * count], refs[2 * count :]
        weights = [
            [ref[:, half].reshape(wide, ref.shape[-1]) for half in range(2)] for ref in pack_refs
        ]
        for segment in range(4):
            total = None
            for left_ref, pair in zip(left_refs, weights):
                for half in range(2):
                    term = nt(left_ref[half, segment * seg : (segment + 1) * seg, :], pair[half])
                    total = term if total is None else total + term
            split_store(split, segment, total)

    cols = [left.shape[-1] for left in lefts]
    half_seg = seg // 2
    return call(
        body,
        split_shapes(seg, width),
        *lefts,
        *packs,
        grid=(planes // group,),
        in_specs=[pl.BlockSpec(left.shape, lambda i: (0, 0, 0)) for left in lefts]
        + [
            pl.BlockSpec((group, 2, rows, c), functools.partial(lambda p, i: (i, 0, 0, p), place))
            for c in cols
        ],
        out_specs=[
            pl.BlockSpec((2, half_seg, wide), lambda i: (0, 0, i)),
            pl.BlockSpec((2, half_seg, wide), lambda i: (0, 0, i)),
            pl.BlockSpec((seg, wide), lambda i: (0, i)),
            pl.BlockSpec((half_seg, wide), lambda i: (0, i)),
            pl.BlockSpec((half_seg, wide), lambda i: (0, i)),
        ],
        flops=2 * 4 * seg * width * 2 * sum(cols),
    )


def weight_grad(which, lefts, right, others, other_right, at, cols, extra, seg):
    width = lefts[0].shape[1]
    wide = 384
    first, second = right.shape[-1], other_right.shape[-1]

    def body(which_ref, *refs):
        left_refs, other_refs, right_ref, other_ref = refs[:5], refs[5:10], refs[10], refs[11]
        out_ref = refs[-1]

        def gathered(places):
            return jnp.concatenate(
                [places[place][:count, :] for place, _, _, count in spans(seg)], axis=0
            )

        def put(low, high, value):
            if extra is not None:
                value = value + refs[12][:, low:high].astype(f32)
            out_ref[:, low:high] = value.astype(bf16)

        put(0, first, tn(gathered(left_refs), right_ref[0]))
        put(at, at + second, tn(gathered(other_refs), other_ref[0]))

    def column(value):
        return pl.BlockSpec((value.shape[0], wide), lambda i, w: (0, i))

    def chosen(value):
        return pl.BlockSpec((1,) + value.shape[1:], lambda i, w: (w[0], 0, 0))

    tile = pl.BlockSpec((wide, cols), lambda i, w: (i, 0))
    args = [*lefts, *others, right, other_right]
    specs = [column(v) for v in (*lefts, *others)] + [chosen(right), chosen(other_right)]
    if extra is not None:
        args.append(extra)
        specs.append(tile)
    return call(
        body,
        [out((width, cols), bf16)],
        which,
        *args,
        grid=(width // wide,),
        in_specs=specs,
        out_specs=[tile],
        prefetch=1,
        flops=2 * 4 * seg * width * cols,
    )[0]


def per_device(
    tokens, starts, w_in, w_out, gate_up, w_down, gain_mix, gain_ffn, conv_taps, cotangent
):
    core = lax.axis_index("mp")
    planes = lax.axis_size("z")
    rows, _, half_c = w_in.shape
    half_f = w_down.shape[0]
    width = tokens.shape[1]
    seg = tokens.shape[0] // 2
    chan, hid = half_c // 4, half_f // 4
    plane_rows = 4 * rows
    tap_len = conv_taps.shape[2]
    tiles = -(-hid // LANES)
    cuts = ((0, tiles // 2 + 1), (tiles // 2 + 1, tiles))
    sizes = [LANES * (high - low) for low, high in cuts]
    own_half = core.astype(jnp.int32).reshape(1)
    other_half = 1 - own_half

    def mine(value):
        return lax.dynamic_slice_in_dim(value, core * seg, seg, axis=0)

    gain_one = gain_mix.astype(f32)[:, None, None]
    gain_two = gain_ffn.astype(f32)[:, None, None]
    in_scaled = (w_in.astype(f32) * gain_one).astype(bf16)
    out_turned = w_out.T

    def conv_columns(q):
        at = slice(q * chan, (q + 1) * chan)
        return [in_scaled[:, 0, at], in_scaled[:, 1, at], out_turned[:, at], in_scaled[:, 2, at]]

    conv_quart = jnp.stack([jnp.concatenate(conv_columns(q), axis=1) for q in range(4)])
    conv_quart = by_xor(conv_quart, plane_bits())
    tap_piece = lax.ppermute(conv_taps.reshape(1, -1), ("z",) + PLANE, taps_turn(False))
    tap_rows = jnp.pad(tap_piece, ((0, 15), (0, 4 * chan - 3 * tap_len)))
    conv_got = exchange_first(conv_quart)

    def over_all(value):
        value = lax.all_gather(value, ("z", "mp"), axis=0, tiled=False)
        return value.reshape((planes, 2) + value.shape[1:])

    inputs = mine(tokens).astype(f32)
    inv_mix = lax.rsqrt(jnp.mean(inputs * inputs, axis=-1, keepdims=True) + epsilon)
    hat_mix = inputs * inv_mix
    begin_row = mine(starts).astype(bf16)[None]
    begin_rows = jnp.pad(begin_row, ((0, 15), (0, width - seg)))
    hat_own = jnp.concatenate([hat_mix.astype(bf16), begin_rows], axis=0)
    hat_own = after(hat_own, conv_quart)
    hat_x, hat_y = gather_first(hat_own)
    conv_pack = exchange_second(after(conv_got, hat_own)).reshape(plane_rows, 4 * chan)
    conv_pack = jnp.concatenate([conv_pack, tap_rows], axis=0)
    conv_all = over_all(conv_pack)
    cot = mine(cotangent)

    place = (2 * lax.axis_index("y") + lax.axis_index("x")).astype(jnp.int32).reshape(1)
    packs = ffn_pack(
        gate_up[:, 0], gate_up[:, 1], w_down.T, gain_two[:, 0], place, cuts, hid
    )
    first_quart, second_quart = packs
    hats = gather_second(hat_own, hat_x, hat_y)
    first_got = exchange_first(first_quart)
    first_pack = exchange_second(after(first_got, hat_x, hat_y)).reshape(plane_rows, -1)
    cot, second_quart = lax.optimization_barrier((cot, second_quart, first_pack, *hats[3:]))[:2]
    second_got = exchange_first(second_quart)
    cot_x, cot_y = gather_first(cot)

    begins = jnp.stack(
        [hats[0][seg, :seg], hats[1][seg, :seg], hats[2][seg, :seg], hats[4][-16, :seg]]
    ).astype(f32)
    earlier = jnp.concatenate([jnp.zeros((4, 1), f32), begins[:, :-1]], axis=1)
    keeps = jnp.stack([1.0 - begins, (1.0 - begins) * (1.0 - earlier)])[..., None]
    last_keep = 1.0 - begins[:, -1:]
    taps = conv_all[:, :, plane_rows, : 3 * tap_len].reshape(planes, 2, 3, tap_len)
    taps = jnp.transpose(taps, (1, 2, 0, 3)).reshape(2, 3, chan).astype(f32)

    b_part, c_part, x_part, mixed_in = conv_project(hats, conv_all, seg)
    tails = mixed_in[:, :, seg - 2 :]
    tail_gate = jnp.stack([last_keep, jnp.ones((4, 1), f32)], axis=1)
    halo = halo_forward((tails * tail_gate).astype(bf16)).astype(f32)
    convolved, gated, mixer = conv_mix(mixed_in, halo, c_part, keeps, taps, conv_all, seg)
    first_in = reduce_first(mixer)
    second_got, cot_x, cot_y = lax.optimization_barrier((second_got, cot_x, cot_y, *mixer))[:3]
    cots = gather_second(cot, cot_x, cot_y)
    second_pack = exchange_second(second_got).reshape(plane_rows, -1)
    ffn_all = [over_all(first_pack), over_all(second_pack)]
    first_in = lax.optimization_barrier((*first_in, second_pack))[:2]
    middle = inputs + reduce_end(mixer, *first_in, *reduce_second(mixer, *first_in))

    inv_ffn = lax.rsqrt(jnp.mean(middle * middle, axis=-1, keepdims=True) + epsilon)
    hat_ffn = middle * inv_ffn
    hats_two = plane_gather(hat_ffn.astype(bf16))

    def other_grad(lefts, right, others, other_right, at, cols):
        theirs = weight_grad(other_half, lefts, right, others, other_right, at, cols, None, seg)
        return core_swap(theirs), theirs

    def own_grad(lefts, right, others, other_right, at, cols, theirs):
        return weight_grad(own_half, lefts, right, others, other_right, at, cols, theirs, seg)

    def over_z(value, *held):
        value = after(value, *held)
        return lax.psum_scatter(value, "z", scatter_dimension=0, tiled=True)

    def cut_grads(acts, grads, size):
        given = (hats_two, grads, cots, acts, 2 * size, 3 * size)
        return own_grad(*given, other_grad(*given))

    done_one = ffn_pass(hats_two, cots, ffn_all[0], sizes[0], seg, (0, 1, 2))
    acts_one, grads_one = ffn_pass(hats_two, cots, ffn_all[0], sizes[0], seg, (3,), done_one)
    given = (hats_two, grads_one, cots, acts_one, 2 * sizes[0], 3 * sizes[0])
    theirs = other_grad(*given)
    second_all = after(ffn_all[1], theirs[1])
    acts_two, grads_two = ffn_pass(hats_two, cots, second_all, sizes[1], seg, (0, 1, 2, 3))
    sum_one = own_grad(*given, after(theirs[0], acts_two))
    red_one = over_z(sum_one)
    grad_hat2 = turned_back(
        [grads_one, after(grads_two, sum_one)], [ffn_all[0], second_all], 0, plane_rows, seg
    )
    acts_two, grads_two = lax.optimization_barrier((acts_two, grads_two, *grad_hat2))[:2]
    given = (hats_two, grads_two, cots, acts_two, 2 * sizes[1], 3 * sizes[1])
    sum_two = own_grad(*given, other_grad(*given)[0])
    red_two = over_z(sum_two)
    first_in = reduce_first(grad_hat2)
    first_in = lax.optimization_barrier((*first_in, sum_two))[:2]
    last_in = reduce_second(grad_hat2, *first_in)
    last_in = lax.optimization_barrier((*last_in, red_one))[:2]
    grad_hat2 = reduce_end(grad_hat2, *first_in, *last_in)
    inner = jnp.mean(grad_hat2 * hat_ffn, axis=-1, keepdims=True)
    grad_middle = cot.astype(f32) + inv_ffn * (grad_hat2 - hat_ffn * inner)

    mixer_own = grad_middle.astype(bf16)
    mixer_x, mixer_y = gather_first(mixer_own)
    ffn_out = turned_back(
        [acts_one, after(acts_two, mixer_own)], [ffn_all[0], second_all], 2, plane_rows, seg
    )
    mixer_x, mixer_y = lax.optimization_barrier((mixer_x, mixer_y, *ffn_out))[:2]
    grad_mixer = gather_second(mixer_own, mixer_x, mixer_y)
    ffn_out = lax.optimization_barrier((*ffn_out, *grad_mixer))[:5]
    grad_c, grad_v, tap_sums, heads = conv_back(
        grad_mixer, mixed_in, halo, c_part, convolved, keeps, taps, conv_all, seg
    )
    back = halo_backward(heads) * tail_gate
    grad_proj = conv_grads(grad_c, grad_v, back, b_part, x_part, keeps, taps, seg)
    gated = gated.reshape(2, 4 * seg, chan)
    given = (hats, grad_proj, grad_mixer, gated, 2 * chan, 4 * chan)
    theirs, sent = other_grad(given[0], after(grad_proj, red_two), *given[2:])
    grad_hat1 = turned_back([after(grad_proj, sent)], [conv_all], 0, plane_rows, seg)
    sum_conv = own_grad(*given, after(theirs, *grad_hat1))
    red_conv = over_z(sum_conv)
    first_in = reduce_first(grad_hat1)
    first_in = lax.optimization_barrier((*first_in, sum_conv))[:2]
    grad_hat1 = reduce_end(grad_hat1, *first_in, *reduce_second(grad_hat1, *first_in))
    inner = jnp.mean(grad_hat1 * hat_mix, axis=-1, keepdims=True)
    grad_inputs = grad_middle + inv_mix * (grad_hat1 - hat_mix * inner)
    output_vals = (middle + plane_reduce(ffn_out)).astype(bf16)

    tap_sums = jnp.where(core == 0, tap_sums, tap_sums[::-1])
    tap_sum = tap_sums[0] + core_swap(tap_sums[1])
    tap_sum = lax.psum(tap_sum, "z").reshape(3, planes, tap_len)
    tap_sum = lax.dynamic_index_in_dim(tap_sum, lax.axis_index("z"), axis=1, keepdims=True)
    tap_grad = lax.ppermute(tap_sum, ("z",) + PLANE, taps_turn(True))

    def owned(value):
        return plane_exchange(value.reshape(4, rows, -1))

    cut_parts = [owned(after(value, sum_conv)) for value in (red_one, red_two)]
    raw_gu = jnp.concatenate(
        [
            part[:, :, : 2 * size].reshape(4, rows, -1, 2, LANES)
            for part, size in zip(cut_parts, sizes)
        ],
        axis=2,
    )
    raw_gu = jnp.transpose(raw_gu, (1, 3, 0, 2, 4)).reshape(rows, 2, 4, tiles * LANES)
    raw_gu = raw_gu[..., :hid].reshape(rows, 2, half_f).astype(f32)
    raw_down = jnp.concatenate(
        [part[:, :, 2 * size :] for part, size in zip(cut_parts, sizes)], axis=2
    )[:, :, :hid]
    out_down = jnp.transpose(raw_down, (0, 2, 1)).reshape(half_f, rows).astype(f32)
    output_vals, grad_inputs = both_cores(output_vals), both_cores(grad_inputs)
    red_conv = after(red_conv, output_vals, grad_inputs, raw_gu, out_down, tap_grad)
    conv_grad = owned(red_conv).astype(f32)

    def conv_cols(k):
        return jnp.concatenate(
            [conv_grad[q, :, k * chan : (k + 1) * chan] for q in range(4)], axis=1
        )

    raw_in = jnp.stack([conv_cols(k) for k in (0, 1, 3)], axis=1)
    gains = jnp.stack(
        [
            jnp.sum(raw_in * w_in.astype(f32), axis=(1, 2)),
            jnp.sum(raw_gu * gate_up.astype(f32), axis=(1, 2)),
        ]
    )
    gains = gains + core_swap(gains)
    return (
        output_vals,
        grad_inputs,
        raw_in * gain_one,
        conv_cols(2).T,
        raw_gu * gain_two,
        out_down,
        gains[0],
        gains[1],
        tap_grad,
    )


def solution(mesh):
    seq, cores = mesh.shape["seq"], mesh.shape["mp"]
    split = Mesh(np.asarray(mesh.devices).reshape(seq // 4, 2, 2, cores), ("z", "y", "x", "mp"))
    by = ("z", "y", "x")
    weights = (
        P(by, None, "mp"),
        P("mp", by),
        P(by, None, "mp"),
        P("mp", by),
        P(by),
        P(by),
        P(None, "mp", by),
    )
    return jax.shard_map(
        per_device,
        mesh=split,
        in_specs=(P(by, None), P(by)) + weights + (P(by, None),),
        out_specs=(P(by, None), P(by, None)) + weights,
        check_vma=False,
    )
```

```python
import functools

import jax
import jax.numpy as jnp
import numpy as np
from jax import lax
from jax.experimental import pallas as pl
from jax.experimental.pallas import tpu as pltpu
from jax.sharding import Mesh, PartitionSpec as P

epsilon = 1e-05
f32 = jnp.float32
bf16 = jnp.bfloat16
PLANE = ("y", "x")
SWAP = ((0, 1), (1, 0))
LANES = 128
VMEM_LIMIT = 50 * 1024 * 1024


def nn(left, right):
    return lax.dot_general(left, right, (((1,), (0,)), ((), ())), preferred_element_type=f32)


def nt(left, right):
    return lax.dot_general(left, right, (((1,), (1,)), ((), ())), preferred_element_type=f32)


def tn(left, right):
    return lax.dot_general(left, right, (((0,), (0,)), ((), ())), preferred_element_type=f32)


def after(value, *others):
    return lax.optimization_barrier((value,) + others)[0]


def together(*groups):
    flat = lax.optimization_barrier(tuple(value for group in groups for value in group))
    ends = np.cumsum([len(group) for group in groups])
    return [list(flat[end - len(group) : end]) for end, group in zip(ends, groups)]


def by_xor(stack, bits):
    places = np.arange(stack.shape[0])
    for level, bit in enumerate(bits):
        turned = jnp.stack([stack[int(p)] for p in places ^ (1 << level)])
        stack = jnp.where(bit, turned, stack)
    return stack


def plane_bits():
    return [lax.axis_index("x") == 1, lax.axis_index("y") == 1]


def plane_swap(value, offset):
    if offset == 1:
        return lax.ppermute(value, "x", SWAP)
    if offset == 2:
        return lax.ppermute(value, "y", SWAP)
    return lax.ppermute(value, PLANE, [(i, i ^ 3) for i in range(4)])


def core_swap(value):
    return lax.ppermute(value, "mp", SWAP)


def exchange_first(relative):
    return [relative[0]] + [plane_swap(relative[r], r) for r in (1, 2, 3)]


def exchange_second(got):
    return by_xor(jnp.stack(got), plane_bits())


def plane_exchange(stack):
    return exchange_second(exchange_first(by_xor(stack, plane_bits())))


def gather_first(top, low):
    return [plane_swap(part, offset) for offset in (1, 2) for part in (top, low)]


def gather_second(near):
    return [plane_swap(near[0], 2), plane_swap(near[3], 1)]


def plane_gather(own):
    half = own.shape[0] // 2
    near = gather_first(own[:half], own[half:])
    return [own] + near + gather_second(near)


def reduce_far(parts):
    return [plane_swap(parts[0], 1), plane_swap(parts[1], 2)]


def reduce_near(parts):
    return [plane_swap(parts[2], 1), plane_swap(parts[3], 2)]


def reduce_passed(parts, far):
    low_on = (parts[6].astype(f32) + far[0].astype(f32)).astype(bf16)
    top_on = (parts[5].astype(f32) + far[1].astype(f32)).astype(bf16)
    return [top_on, low_on], [plane_swap(top_on, 1), plane_swap(low_on, 2)]


def halo_forward(tails):
    planes = lax.axis_size("z")
    got = core_swap(tails)
    jump = [(2 * z + 1, 2 * z + 2) for z in range(planes - 1)]
    ordered = by_xor(jnp.moveaxis(tails, 1, 0), plane_bits())
    before = lax.ppermute(ordered[3], ("z", "mp"), jump)
    ordered = by_xor(jnp.moveaxis(got, 1, 0), plane_bits())
    shifted = by_xor(jnp.concatenate([before[None], ordered[:3]], axis=0), plane_bits())
    return jnp.where(lax.axis_index("mp") == 1, got, jnp.moveaxis(shifted, 0, 1))


def halo_backward(heads):
    planes = lax.axis_size("z")
    got = core_swap(heads)
    jump = [(2 * z + 2, 2 * z + 1) for z in range(planes - 1)]
    ordered = by_xor(jnp.moveaxis(heads, 1, 0), plane_bits())
    behind = lax.ppermute(ordered[0], ("z", "mp"), jump)
    ordered = by_xor(jnp.moveaxis(got, 1, 0), plane_bits())
    shifted = by_xor(jnp.concatenate([ordered[1:], behind[None]], axis=0), plane_bits())
    return jnp.where(lax.axis_index("mp") == 1, jnp.moveaxis(shifted, 0, 1), got)


def taps_turn(back):
    planes = lax.axis_size("z")
    pairs = [(s, (s % planes) * 4 + s // planes) for s in range(4 * planes)]
    return [(b, a) for a, b in pairs] if back else pairs


def call(body, out_shapes, *args, grid=None, in_specs=None, out_specs=None, prefetch=0, flops=0, aliases=None):
    def whole(value):
        zeros = (0,) * len(value.shape)
        return pl.BlockSpec(value.shape, lambda *_: zeros)

    if in_specs is None:
        in_specs = [whole(value) for value in args[prefetch:]]
    if out_specs is None:
        out_specs = [whole(value) for value in out_shapes]
    moved = sum(a.size * a.dtype.itemsize for a in args)
    moved += sum(o.size * o.dtype.itemsize for o in out_shapes)
    return pl.pallas_call(
        body,
        out_shape=out_shapes,
        grid_spec=pltpu.PrefetchScalarGridSpec(
            num_scalar_prefetch=prefetch,
            grid=grid or (1,),
            in_specs=in_specs,
            out_specs=out_specs,
        ),
        input_output_aliases=aliases or {},
        compiler_params=pltpu.CompilerParams(vmem_limit_bytes=VMEM_LIMIT),
        cost_estimate=pl.CostEstimate(flops=flops // 10000, bytes_accessed=moved // 10000, transcendentals=0),
    )(*args)


def out(shape, dtype):
    return jax.ShapeDtypeStruct(shape, dtype)


def spans(seg):
    half = seg // 2
    parts = [(0, 0, 0, seg)]
    for segment in (1, 2, 3):
        parts.append((2 * segment - 1, segment, 0, half))
        parts.append((2 * segment, segment, half, seg - half))
    return parts


BLOCKS = 7


def split_shapes(seg, width):
    half = seg // 2
    return [out((seg if place == 4 else half, width), bf16) for place in range(BLOCKS)]


def split_store(refs, segment, value):
    value = value.astype(bf16)
    half = value.shape[0] // 2
    if segment == 0:
        refs[4][...] = value
        return
    top, low = {1: (5, 2), 2: (3, 6), 3: (1, 0)}[segment]
    refs[top][...] = value[:half]
    refs[low][...] = value[half:]


def conv_project(hats, pack, seg, tap_len):
    planes, _, rows_taps, cols = pack.shape
    rows, chan = rows_taps - 16, cols // 4
    width = planes * rows

    def body(*refs):
        hat_refs, pack_ref = refs[:BLOCKS], refs[BLOCKS]
        b_ref, c_ref, x_ref, u_ref, keep_ref, taps_ref, tails_ref, gate_ref = refs[BLOCKS + 1 :]
        for segment, place in enumerate((0, 2, 4, 6)):
            below = hat_refs[place].shape[0] - 16
            begins = hat_refs[place][below:, :seg].astype(f32)[0:1]
            begins = jnp.transpose(jnp.broadcast_to(begins, (LANES, seg)))
            before = jnp.where(rows_of((seg, LANES)) == 0, 0.0, pltpu.roll(begins, 1, 0))
            keep_one = (1.0 - begins)[:, :1]
            keep_ref[0, segment] = keep_one
            keep_ref[1, segment] = ((1.0 - begins) * (1.0 - before))[:, :1]
            gate_ref[segment, 0:1] = keep_one[seg - 1 :]
            gate_ref[segment, 1:2] = jnp.ones((1, 1), f32)
        for half in range(2):
            weights = pack_ref[:, half, :rows, :].reshape(width, cols)
            for plane in range(planes):
                row = pack_ref[plane, half, rows:, :].astype(f32)[0:1]
                for k in range(3):
                    at = pl.ds(plane * tap_len, tap_len)
                    taps_ref[half, k : k + 1, at] = row[:, k * tap_len : (k + 1) * tap_len]
            for place, segment, low, count in spans(seg):
                proj = nn(hat_refs[place][:count, :], weights)
                b_val, c_val, x_val = (
                    proj[:, :chan],
                    proj[:, chan : 2 * chan],
                    proj[:, 3 * chan :],
                )
                at = (half, segment, pl.ds(low, count))
                b_ref[at] = b_val
                c_ref[at] = c_val
                x_ref[at] = x_val
                u_val = b_val * x_val
                u_ref[at] = u_val.astype(bf16)
                if low + count == seg:
                    last = u_val[count - 2 :].astype(bf16).astype(f32) * gate_ref[segment]
                    tails_ref[half, segment] = last.astype(bf16)

    shape = (2, 4, seg, chan)
    results = call(
        body,
        [out(shape, f32)] * 3
        + [out(shape, bf16), out((2, 4, seg, 1), f32), out((2, 3, chan), f32)]
        + [out((2, 4, 2, chan), bf16), out((4, 2, 1), f32)],
        *hats,
        pack,
        flops=2 * 4 * seg * width * cols * 2,
    )
    return results[:4], results[4:]


def rows_of(shape):
    return lax.broadcasted_iota(jnp.int32, shape, 0)


def earlier_rows(value, halo):
    row = rows_of(value.shape)
    one = jnp.where(row == 0, halo[1:2], pltpu.roll(value, 1, 0))
    two = jnp.where(row == 0, halo[0:1], jnp.where(row == 1, halo[1:2], pltpu.roll(value, 2, 0)))
    return one, two


def conv_mix(u_vals, halo, c_part, keeps, taps, pack, seg):
    planes, _, rows_taps, cols = pack.shape
    rows, chan = rows_taps - 16, cols // 4
    width = planes * rows

    def body(u_ref, halo_ref, c_ref, keep_ref, taps_ref, pack_ref, v_ref, y_ref, *split):
        outs = [
            pack_ref[:, half, :rows, 2 * chan : 3 * chan].reshape(width, chan) for half in range(2)
        ]
        for segment in range(4):
            keep_one, keep_two = keep_ref[0, segment], keep_ref[1, segment]
            total = None
            for half in range(2):
                u_val = u_ref[half, segment].astype(f32)
                one, two = earlier_rows(u_val, halo_ref[half, segment])
                tap = taps_ref[half]
                v_val = tap[0:1] * u_val + tap[1:2] * keep_one * one + tap[2:3] * keep_two * two
                y_val = (c_ref[half, segment] * v_val).astype(bf16)
                v_ref[half, segment] = v_val
                y_ref[half, segment] = y_val
                term = nt(y_val, outs[half])
                total = term if total is None else total + term
            split_store(split, segment, total)

    shape = (2, 4, seg, chan)
    results = call(
        body,
        [out(shape, f32), out(shape, bf16)] + split_shapes(seg, width),
        u_vals,
        halo,
        c_part,
        keeps,
        taps,
        pack,
        flops=2 * 4 * seg * width * 2 * chan,
    )
    return results[0], results[1], results[2:]


def conv_back(grad_mixer, u_vals, halo, c_part, v_vals, keeps, taps, pack, seg):
    planes, _, rows_taps, cols = pack.shape
    rows, chan = rows_taps - 16, cols // 4
    width = planes * rows

    def body(*refs):
        mix_refs, refs = refs[:BLOCKS], refs[BLOCKS:]
        u_ref, halo_ref, c_ref, v_ref, keep_ref, taps_ref, pack_ref = refs[:7]
        dc_ref, dv_ref, sums_ref, heads_ref = refs[7:]
        for half in range(2):
            outs = pack_ref[:, half, :rows, 2 * chan : 3 * chan].reshape(width, chan)
            for place, segment, low, count in spans(seg):
                at = (half, segment, pl.ds(low, count))
                grad_y = nn(mix_refs[place][:count, :], outs)
                dc_ref[at] = (grad_y * v_ref[at]).astype(bf16)
                dv_ref[at] = grad_y * c_ref[at]
            sums = [jnp.zeros((1, chan), f32)] * 3
            tap = taps_ref[half]
            for segment in range(4):
                keep_one, keep_two = keep_ref[0, segment], keep_ref[1, segment]
                u_val = u_ref[half, segment].astype(f32)
                one, two = earlier_rows(u_val, halo_ref[half, segment])
                grad_v = dv_ref[half, segment]
                once, twice = keep_one * grad_v, keep_two * grad_v
                for k, term in enumerate((grad_v * u_val, once * one, twice * two)):
                    sums[k] = sums[k] + jnp.sum(term, axis=0, keepdims=True)
                heads_ref[half, segment, 0:1] = tap[2:3] * twice[0:1]
                heads_ref[half, segment, 1:2] = tap[1:2] * once[0:1] + tap[2:3] * twice[1:2]
            for k in range(3):
                sums_ref[half, k : k + 1] = sums[k]

    shape = (2, 4, seg, chan)
    return call(
        body,
        [out(shape, bf16), out(shape, f32), out((2, 3, chan), f32), out((2, 4, 2, chan), f32)],
        *grad_mixer,
        u_vals,
        halo,
        c_part,
        v_vals,
        keeps,
        taps,
        pack,
        flops=2 * 4 * seg * width * 2 * chan,
    )


def conv_grads(grad_c, grad_v, back, b_part, x_part, keeps, taps, seg):
    chan = grad_v.shape[-1]

    def body(dc_ref, dv_ref, back_ref, b_ref, x_ref, keep_ref, taps_ref, dp_ref):
        row = rows_of((seg, chan))
        for segment in range(4):
            keep_one, keep_two = keep_ref[0, segment], keep_ref[1, segment]
            for half in range(2):
                tap = taps_ref[half]
                grad_val = dv_ref[half, segment]
                once = jnp.where(row == seg - 1, 0.0, pltpu.roll(keep_one * grad_val, seg - 1, 0))
                twice = jnp.where(row >= seg - 2, 0.0, pltpu.roll(keep_two * grad_val, seg - 2, 0))
                grad_u = tap[0:1] * grad_val + tap[1:2] * once + tap[2:3] * twice
                ends = back_ref[half, segment]
                grad_u = grad_u + jnp.where(
                    row == seg - 2, ends[0:1], jnp.where(row == seg - 1, ends[1:2], 0.0)
                )
                grad_u = grad_u.astype(bf16).astype(f32)
                dp_ref[half, segment * seg : (segment + 1) * seg, :] = jnp.concatenate(
                    [
                        grad_u * x_ref[half, segment],
                        dc_ref[half, segment].astype(f32),
                        jnp.zeros((seg, chan), f32),
                        grad_u * b_ref[half, segment],
                    ],
                    axis=1,
                ).astype(bf16)

    return call(
        body,
        [out((2, 4 * seg, 4 * chan), bf16)],
        grad_c,
        grad_v,
        back,
        b_part,
        x_part,
        keeps,
        taps,
    )[0]


def ffn_pack(gate, up, down, gain, place, cuts, chan_hid):
    rows = gate.shape[0]
    hid = chan_hid

    def body(place_ref, gate_ref, up_ref, down_ref, gain_ref, *outs):
        scale = gain_ref[...]
        for q in range(4):
            for (low, high), out_ref in zip(cuts, outs):
                tiles = high - low
                for t in range(tiles):
                    start = (low + t) * LANES
                    count = min(hid - start, LANES)
                    values = [
                        ref[:, q * hid + start : q * hid + start + count]
                        for ref in (gate_ref, up_ref, down_ref)
                    ]
                    values[0] = (values[0].astype(f32) * scale).astype(bf16)
                    values[1] = (values[1].astype(f32) * scale).astype(bf16)
                    if count < LANES:
                        fill = jnp.zeros((rows, LANES - count), bf16)
                        values = [jnp.concatenate([v, fill], axis=1) for v in values]
                    for value, column in zip(values, (2 * t, 2 * t + 1, 2 * tiles + t)):
                        out_ref[q ^ place_ref[0], :, column * LANES : (column + 1) * LANES] = value

    return call(
        body,
        [out((4, rows, 3 * LANES * (high - low)), bf16) for low, high in cuts],
        place,
        gate,
        up,
        down,
        gain,
        prefetch=1,
    )


def ffn_unpack(first, second, gate, up, gain, place, cuts, chan_hid):
    rows, half_f = gate.shape
    hid = chan_hid

    def body(place_ref, first_ref, second_ref, gate_ref, up_ref, gain_ref, gu_ref, down_ref, sum_ref):
        scale = gain_ref[...]
        total = jnp.zeros((rows, LANES), f32)
        for q in range(4):
            for (low, high), ref in zip(cuts, (first_ref, second_ref)):
                tiles = high - low
                for t in range(tiles):
                    start = (low + t) * LANES
                    count = min(hid - start, LANES)
                    at = q * hid + start
                    values = [
                        ref[q ^ place_ref[0], :, column * LANES : (column + 1) * LANES].astype(f32)
                        for column in (2 * t, 2 * t + 1, 2 * tiles + t)
                    ]
                    for side, w_ref in enumerate((gate_ref, up_ref)):
                        weight = w_ref[:, at : at + count].astype(f32)
                        if count < LANES:
                            fill = jnp.zeros((rows, LANES - count), f32)
                            weight = jnp.concatenate([weight, fill], axis=1)
                        total = total + values[side] * weight
                        base = side * half_f + at
                        gu_ref[:, base : base + count] = (values[side] * scale)[:, :count]
                    down_ref[:, at : at + count] = values[2][:, :count]
        sum_ref[...] = jnp.sum(total, axis=1, keepdims=True)

    return call(
        body,
        [out((rows, 2 * half_f), f32), out((rows, half_f), f32), out((rows, 1), f32)],
        place,
        first,
        second,
        gate,
        up,
        gain,
        prefetch=1,
    )


def ffn_pass(hats, cots, pack, size, seg, segments, earlier=None):
    planes, _, rows, _ = pack.shape
    width = planes * rows
    tiles = size // LANES
    blocks = [span for span in spans(seg) if span[1] in segments]
    hats, cots = ([values[span[0]] for span in blocks] for values in (hats, cots))
    count_in = len(blocks)
    first = blocks[0][1]
    held_rows = len(segments) * seg

    def body(*refs):
        hat_refs, cot_refs = refs[:count_in], refs[count_in : 2 * count_in]
        gu_ref, down_ref = refs[2 * count_in : 2 * count_in + 2]
        a_ref, dg_ref = refs[-2:]
        downs = jnp.concatenate(
            [down_ref[:, half].reshape(width, LANES) for half in range(2)], axis=1
        )
        gus = [gu_ref[:, half].reshape(width, 2 * LANES) for half in range(2)]
        for hat_ref, cot_ref, (_, segment, low, count) in zip(hat_refs, cot_refs, blocks):
            at = pl.ds((segment - first) * seg + low, count)
            grad_act = nn(cot_ref[:count, :], downs)
            for half in range(2):
                vals = nn(hat_ref[:count, :], gus[half])
                gate, up = vals[:, :LANES], vals[:, LANES:]
                grad = grad_act[:, half * LANES : (half + 1) * LANES]
                sig = 1.0 / (1.0 + jnp.exp(-gate))
                silu = gate * sig
                a_ref[half, at, :] = (silu * up).astype(bf16)
                dg_ref[half, at, :LANES] = (grad * up * (sig + silu * (1.0 - sig))).astype(bf16)
                dg_ref[half, at, LANES:] = (grad * silu).astype(bf16)

    def held(value):
        return pl.BlockSpec(value.shape, lambda t: (0, 0))

    tokens = 4 * seg
    place = first * seg // held_rows
    args = [*hats, *cots, pack, pack]
    specs = [held(v) for v in (*hats, *cots)] + [
        pl.BlockSpec((planes, 2, rows, 2 * LANES), lambda t: (0, 0, 0, t)),
        pl.BlockSpec((planes, 2, rows, LANES), lambda t: (0, 0, 0, 2 * tiles + t)),
    ]
    aliases = None
    if earlier is not None:
        aliases = {len(args): 0, len(args) + 1: 1}
        args += list(earlier)
        specs += [pl.BlockSpec(memory_space=pl.ANY)] * 2
    return call(
        body,
        [out((2, tokens, size), bf16), out((2, tokens, 2 * size), bf16)],
        *args,
        grid=(tiles,),
        in_specs=specs,
        out_specs=[
            pl.BlockSpec((2, held_rows, LANES), lambda t: (0, place, t)),
            pl.BlockSpec((2, held_rows, 2 * LANES), lambda t: (0, place, t)),
        ],
        flops=2 * held_rows * width * 6 * size,
        aliases=aliases,
    )


def turned_back(lefts, packs, place, rows, seg):
    planes = packs[0].shape[0]
    width = planes * rows
    group = max(1, 2 * planes // 4)
    wide = group * rows

    def body(*refs):
        count = len(lefts)
        left_refs, pack_refs, split = refs[:count], refs[count : 2 * count], refs[2 * count :]
        weights = [
            [ref[:, half].reshape(wide, ref.shape[-1]) for half in range(2)] for ref in pack_refs
        ]
        for segment in range(4):
            total = None
            for left_ref, pair in zip(left_refs, weights):
                for half in range(2):
                    term = nt(left_ref[half, segment * seg : (segment + 1) * seg, :], pair[half])
                    total = term if total is None else total + term
            split_store(split, segment, total)

    cols = [left.shape[-1] for left in lefts]
    shapes = split_shapes(seg, width)
    return call(
        body,
        shapes,
        *lefts,
        *packs,
        grid=(planes // group,),
        in_specs=[pl.BlockSpec(left.shape, lambda i: (0, 0, 0)) for left in lefts]
        + [
            pl.BlockSpec((group, 2, rows, c), functools.partial(lambda p, i: (i, 0, 0, p), place))
            for c in cols
        ],
        out_specs=[pl.BlockSpec((shape.shape[0], wide), lambda i: (0, i)) for shape in shapes],
        flops=2 * 4 * seg * width * 2 * sum(cols),
    )


def weight_grad(lefts, right, others, other_right, at, rows, seg, extra=None):
    width = lefts[0].shape[1]
    wide = 384
    group = wide // rows
    first, second = right.shape[-1], other_right.shape[-1]
    cols = max(first, at + second)
    below = 0 if extra is None else extra.shape[2]

    def body(*refs):
        left_refs, other_refs, refs = refs[:BLOCKS], refs[BLOCKS : 2 * BLOCKS], refs[2 * BLOCKS :]
        right_ref, other_ref, out_ref = refs[0], refs[1], refs[-1]

        def gathered(places):
            return jnp.concatenate(
                [places[place][:count, :] for place, _, _, count in spans(seg)], axis=0
            )

        def put(low, value):
            value = value.astype(bf16).reshape(group, rows, value.shape[-1])
            out_ref[:, 0, :rows, low : low + value.shape[-1]] = value

        put(0, tn(gathered(left_refs), right_ref[0]))
        put(at, tn(gathered(other_refs), other_ref[0]))
        if extra is not None:
            out_ref[:, 0, rows:, :] = refs[2][:, 0]

    def column(value):
        return pl.BlockSpec((value.shape[0], wide), lambda h, i: (0, i))

    def chosen(value):
        return pl.BlockSpec((1,) + value.shape[1:], lambda h, i: (h, 0, 0))

    args = [*lefts, *others, right, other_right]
    specs = [column(v) for v in (*lefts, *others)] + [chosen(right), chosen(other_right)]
    if extra is not None:
        args.append(extra)
        specs.append(pl.BlockSpec((group, 1, below, cols), lambda h, i: (i, h, 0, 0)))
    return call(
        body,
        [out((width // rows, 2, rows + below, cols), bf16)],
        *args,
        grid=(2, width // wide),
        in_specs=specs,
        out_specs=[
            pl.BlockSpec((group, 1, rows + below, cols), lambda h, i: (i, h, 0, 0)),
        ],
        flops=2 * 4 * seg * width * cols * 2,
    )[0]


def sum_parts(own_ref, last_refs):
    top_passed, low_passed, low_near, top_near = [ref[...].astype(f32) for ref in last_refs]
    half = top_near.shape[0]
    own = own_ref[...].astype(f32)
    return jnp.concatenate(
        [own[:half] + top_near + top_passed, own[half:] + low_near + low_passed], axis=0
    )


def halves(shape, dtype):
    return [out((shape[0] // 2,) + shape[1:], dtype)] * 2


def store_halves(value, refs):
    half = value.shape[0] // 2
    refs[0][...] = value[:half]
    refs[1][...] = value[half:]


def middle_norm(parts, last, tokens, core):
    rows, width = parts[4].shape

    def body(core_ref, own_ref, *refs):
        last_refs, token_ref, mid_ref, inv_ref, hat_ref, *half_refs = refs[:4], *refs[4:]
        middle = token_ref[...].astype(f32) + sum_parts(own_ref, last_refs)
        inv = lax.rsqrt(jnp.mean(middle * middle, axis=-1, keepdims=True) + epsilon)
        hat = (middle * inv).astype(bf16)
        mid_ref[...] = middle
        inv_ref[...] = inv
        hat_ref[...] = hat
        store_halves(hat, half_refs)

    shape = (rows, width)
    return on_core(
        body,
        [out(shape, f32), out((rows, 1), f32), out(shape, bf16)] + halves(shape, bf16),
        core,
        [parts[4], *last],
        [tokens],
    )


def middle_back(parts, last, middle, inv, cot, core):
    rows, width = parts[4].shape

    def body(core_ref, own_ref, *refs):
        last_refs, mid_ref, inv_ref, cot_ref, grad_ref, round_ref, *half_refs = (
            refs[:4],
            *refs[4:],
        )
        grad = sum_parts(own_ref, last_refs)
        inv = inv_ref[...]
        hat = mid_ref[...] * inv
        inner = jnp.mean(grad * hat, axis=-1, keepdims=True)
        grad = cot_ref[...].astype(f32) + inv * (grad - hat * inner)
        grad_ref[...] = grad
        rounded = grad.astype(bf16)
        round_ref[...] = rounded
        store_halves(rounded, half_refs)

    shape = (rows, width)
    return on_core(
        body,
        [out(shape, f32), out(shape, bf16)] + halves(shape, bf16),
        core,
        [parts[4], *last, middle, inv, cot],
        [],
    )


def on_core(body, shapes, core, args, by_core, both=()):
    def whole(value):
        zeros = (0,) * len(value.shape)
        return pl.BlockSpec(value.shape, lambda i, c: zeros)

    def part(value):
        return pl.BlockSpec((value.shape[0] // 2, value.shape[1]), lambda i, c: (c[0], 0))

    return call(
        body,
        list(shapes) + list(both),
        core,
        *args,
        *by_core,
        in_specs=[whole(v) for v in args] + [part(v) for v in by_core],
        out_specs=[whole(v) for v in shapes] + [part(v) for v in both],
        prefetch=1,
    )


def block_out(parts, last, middle, core):
    rows, width = middle.shape

    def body(core_ref, own_ref, *refs):
        last_refs, mid_ref, result_ref, both_ref = refs[:4], *refs[4:]
        result = (mid_ref[...] + sum_parts(own_ref, last_refs)).astype(bf16)
        result_ref[...] = result
        both_ref[...] = result

    return on_core(
        body,
        [out((rows, width), bf16)],
        core,
        [parts[4], *last, middle],
        [],
        [out((2 * rows, width), bf16)],
    )


def tokens_back(parts, last, grad_middle, tokens, core):
    rows, width = grad_middle.shape

    def body(core_ref, own_ref, *refs):
        last_refs, grad_ref, token_ref, result_ref, both_ref = refs[:4], *refs[4:]
        grad = sum_parts(own_ref, last_refs)
        values = token_ref[...].astype(f32)
        inv = lax.rsqrt(jnp.mean(values * values, axis=-1, keepdims=True) + epsilon)
        hat = values * inv
        inner = jnp.mean(grad * hat, axis=-1, keepdims=True)
        result = grad_ref[...] + inv * (grad - hat * inner)
        result_ref[...] = result
        both_ref[...] = result

    return on_core(
        body,
        [out((rows, width), f32)],
        core,
        [parts[4], *last, grad_middle],
        [tokens],
        [out((2 * rows, width), f32)],
    )


def fill_other(both, other, core):
    rows, width = other.shape

    def body(core_ref, other_ref, _, both_ref):
        both_ref[...] = other_ref[...]

    return call(
        body,
        [out(both.shape, both.dtype)],
        core,
        other,
        both,
        in_specs=[
            pl.BlockSpec((rows, width), lambda i, c: (0, 0)),
            pl.BlockSpec(memory_space=pl.ANY),
        ],
        out_specs=[pl.BlockSpec((rows, width), lambda i, c: (1 - c[0], 0))],
        prefetch=1,
        aliases={2: 0},
    )[0]


def per_device(
    tokens, starts, w_in, w_out, gate_up, w_down, gain_mix, gain_ffn, conv_taps, cotangent
):
    core = lax.axis_index("mp")
    planes = lax.axis_size("z")
    rows, _, half_c = w_in.shape
    half_f = w_down.shape[0]
    width = tokens.shape[1]
    seg = tokens.shape[0] // 2
    chan, hid = half_c // 4, half_f // 4
    plane_rows = 4 * rows
    tap_len = conv_taps.shape[2]
    tiles = -(-hid // LANES)
    cuts = ((0, tiles // 2 + 1), (tiles // 2 + 1, tiles))
    sizes = [LANES * (high - low) for low, high in cuts]
    own_half = core.astype(jnp.int32).reshape(1)

    def mine(value):
        return lax.dynamic_slice_in_dim(value, core * seg, seg, axis=0)

    gain_one = gain_mix.astype(f32)[:, None, None]
    gain_two = gain_ffn.astype(f32)[:, None, None]
    in_scaled = (w_in.astype(f32) * gain_one).astype(bf16)
    out_turned = w_out.T

    def conv_columns(q):
        at = slice(q * chan, (q + 1) * chan)
        return [in_scaled[:, 0, at], in_scaled[:, 1, at], out_turned[:, at], in_scaled[:, 2, at]]

    conv_quart = jnp.stack([jnp.concatenate(conv_columns(q), axis=1) for q in range(4)])
    conv_quart = by_xor(conv_quart, plane_bits())
    tap_piece = lax.ppermute(conv_taps.reshape(1, -1), ("z",) + PLANE, taps_turn(False))
    tap_rows = jnp.pad(tap_piece, ((0, 15), (0, 4 * chan - 3 * tap_len)))
    conv_got = exchange_first(conv_quart)

    def over_all(value):
        value = lax.all_gather(value, ("z", "mp"), axis=0, tiled=False)
        return value.reshape((planes, 2) + value.shape[1:])

    inputs = mine(tokens).astype(f32)
    inv_mix = lax.rsqrt(jnp.mean(inputs * inputs, axis=-1, keepdims=True) + epsilon)
    hat_mix = inputs * inv_mix
    hat_own = hat_mix.astype(bf16)
    begin_rows = jnp.pad(mine(starts).astype(bf16)[None], ((0, 15), (0, width - seg)))
    half_seg = seg // 2
    hat_low = jnp.concatenate([hat_own[half_seg:], begin_rows], axis=0)
    hat_top = hat_own[:half_seg]
    hat_own = jnp.concatenate([hat_own, begin_rows], axis=0)
    hat_own, hat_top, hat_low = lax.optimization_barrier((hat_own, hat_top, hat_low, conv_quart))[:3]
    hats_near = gather_first(hat_top, hat_low)
    conv_pack = exchange_second(after(conv_got, hat_own)).reshape(plane_rows, 4 * chan)
    conv_pack = jnp.concatenate([conv_pack, tap_rows], axis=0)
    conv_all = over_all(conv_pack)
    cot = mine(cotangent)

    place = (2 * lax.axis_index("y") + lax.axis_index("x")).astype(jnp.int32).reshape(1)
    packs = ffn_pack(
        gate_up[:, 0], gate_up[:, 1], w_down.T, gain_two[:, 0], place, cuts, hid
    )
    first_quart, second_quart = packs
    first_got = exchange_first(first_quart)
    hats_near, first_got = together(hats_near, first_got)
    hats = [hat_own] + hats_near + gather_second(hats_near)
    first_pack = exchange_second(first_got).reshape(plane_rows, -1)
    cot, cot_top, cot_low = lax.optimization_barrier(
        (cot, cot[:half_seg], cot[half_seg:], *hats[5:])
    )[:3]
    cots_near = gather_first(cot_top, cot_low)

    projected, marks = conv_project(hats, conv_all, seg, tap_len)
    projected, marks, cots_near, (second_quart,) = together(
        projected, marks, cots_near, (second_quart,)
    )
    b_part, c_part, x_part, mixed_in = projected
    keeps, taps, tails, tail_gate = marks
    second_got = exchange_first(second_quart)
    halo = halo_forward(tails).astype(f32)
    convolved, gated, mixer = conv_mix(mixed_in, halo, c_part, keeps, taps, conv_all, seg)
    mixer, second_got = together(mixer, second_got)
    far, near = reduce_far(mixer), reduce_near(mixer)
    second_pack = exchange_second(second_got).reshape(plane_rows, -1)
    ffn_all = [over_all(first_pack), over_all(second_pack)]
    far, near, mixer, _ = together(far, near, mixer, (second_pack,))
    passed = reduce_passed(mixer, far)[1]
    last, mixer = together(passed + near, mixer)
    middle, inv_ffn, hat_own, hat_top, hat_low = middle_norm(mixer, last, tokens, own_half)

    near = gather_first(hat_top, hat_low)

    def first_cut(segment, earlier):
        return ffn_pass(hats_two, cots, ffn_all[0], sizes[0], seg, (segment,), earlier)

    hats_two, cots = [hat_own], [cot] + cots_near
    done_one = first_cut(0, None)
    done_one, near, cots_near = together(done_one, near, cots_near)
    hats_two, cots = [hat_own] + near, [cot] + cots_near
    far, cots_far = gather_second(near), gather_second(cots_near)
    done_one = first_cut(2, first_cut(1, done_one))
    done_one, far, cots_far = together(done_one, far, cots_far)
    hats_two, cots = hats_two + far, cots + cots_far

    def ordered(value):
        stack = by_xor(value.reshape(4, rows, -1), plane_bits())
        return [stack[r] for r in range(4)]

    def over_owners(value):
        value = value.reshape((2 * planes,) + value.shape[2:])
        return lax.psum_scatter(value, ("z", "mp"), scatter_dimension=0, tiled=False)

    acts_one, grads_one = first_cut(3, done_one)
    sum_one = weight_grad(hats_two, grads_one, cots, acts_one, 2 * sizes[0], plane_rows, seg)
    red_one = over_owners(sum_one)
    second_all = after(ffn_all[1], sum_one)
    acts_two, grads_two = ffn_pass(hats_two, cots, second_all, sizes[1], seg, (0, 1, 2, 3))
    grad_hat2 = turned_back([grads_one, grads_two], [ffn_all[0], second_all], 0, plane_rows, seg)
    far, near = reduce_far(grad_hat2), reduce_near(grad_hat2)
    acts_two, grads_two = lax.optimization_barrier((acts_two, grads_two, *grad_hat2))[:2]
    sum_two = weight_grad(hats_two, grads_two, cots, acts_two, 2 * sizes[1], plane_rows, seg)
    far, near, grad_hat2, (sum_two,) = together(far, near, grad_hat2, (sum_two,))
    red_two = over_owners(sum_two)
    sent, passed = reduce_passed(grad_hat2, far)
    acts_last = lax.optimization_barrier((acts_two, *sent))[0]
    ffn_out = turned_back([acts_one, acts_last], [ffn_all[0], second_all], 2, plane_rows, seg)
    last, ffn_out, grad_hat2 = together(passed + near, ffn_out, grad_hat2)
    grad_middle, mix_own, mix_top, mix_low = middle_back(
        grad_hat2, last, middle, inv_ffn, cot, own_half
    )

    near = gather_first(mix_top, mix_low)
    near, (back_one,) = together(near, (red_one,))
    grad_mixer = [mix_own] + near + gather_second(near)
    ffn_out, grad_mixer = together(ffn_out, grad_mixer)
    ffn_far = reduce_far(ffn_out)
    grad_c, grad_v, tap_sums, heads = conv_back(
        grad_mixer, mixed_in, halo, c_part, convolved, keeps, taps, conv_all, seg
    )
    (heads,), ffn_far, ffn_out = together((heads,), ffn_far, ffn_out)
    ffn_passed = reduce_passed(ffn_out, ffn_far)[1]
    back = halo_backward(heads) * tail_gate
    grad_proj = conv_grads(grad_c, grad_v, back, b_part, x_part, keeps, taps, seg)
    (grad_proj,), ffn_passed, back_one = together((grad_proj,), ffn_passed, ordered(back_one))
    first_got = exchange_first(back_one)
    ffn_near = reduce_near(ffn_out)
    gated = gated.reshape(2, 4 * seg, chan)
    tap_rows = jnp.transpose(tap_sums.reshape(2, 3, planes, tap_len), (2, 0, 1, 3))
    tap_rows = tap_rows.reshape(planes, 2, 1, 3 * tap_len).astype(bf16)
    tap_rows = jnp.pad(tap_rows, ((0, 0), (0, 0), (0, 15), (0, 4 * chan - 3 * tap_len)))
    sum_conv = weight_grad(
        hats, grad_proj, grad_mixer, gated, 2 * chan, plane_rows, seg, tap_rows
    )
    red_conv = over_owners(sum_conv)
    (grad_proj,), ffn_near, _ = together((grad_proj,), ffn_near, (sum_conv,))
    grad_hat1 = turned_back([grad_proj], [conv_all], 0, plane_rows, seg)
    grad_hat1, first_got, back_two = together(grad_hat1, first_got, ordered(red_two))
    far, near = reduce_far(grad_hat1), reduce_near(grad_hat1)
    out_own, out_both = block_out(ffn_out, ffn_passed + ffn_near, middle, own_half)
    far, near, grad_hat1, (out_own, out_both) = together(far, near, grad_hat1, (out_own, out_both))
    sent, passed = reduce_passed(grad_hat1, far)
    back_two, _ = together(back_two, sent)
    second_got = exchange_first(back_two)
    output_vals = fill_other(out_both, core_swap(after(out_own, *sent)), own_half)

    out_gu, down_turned, gain_sum = ffn_unpack(
        jnp.stack(first_got),
        jnp.stack(second_got),
        gate_up[:, 0],
        gate_up[:, 1],
        gain_two[:, 0],
        place,
        cuts,
        hid,
    )
    out_gu = out_gu.reshape(rows, 2, half_f)
    out_down = down_turned.T
    conv_got = exchange_first(ordered(red_conv[:plane_rows]))
    last, grad_hat1, conv_got, (out_gu, out_down, gain_sum, output_vals) = together(
        passed + near, grad_hat1, conv_got, (out_gu, out_down, gain_sum, output_vals)
    )
    grad_own, grad_both = tokens_back(grad_hat1, last, grad_middle, tokens, own_half)
    grad_inputs = fill_other(grad_both, core_swap(grad_own), own_half)
    conv_grad = exchange_second(conv_got).astype(f32)
    tap_grad = lax.ppermute(
        red_conv[plane_rows, : 3 * tap_len].astype(f32).reshape(3, 1, tap_len),
        ("z",) + PLANE,
        taps_turn(True),
    )

    def conv_cols(k):
        return jnp.concatenate(
            [conv_grad[q, :, k * chan : (k + 1) * chan] for q in range(4)], axis=1
        )

    raw_in = jnp.stack([conv_cols(k) for k in (0, 1, 3)], axis=1)
    gains = jnp.stack(
        [
            jnp.sum(raw_in * w_in.astype(f32), axis=(1, 2)),
            gain_sum[:, 0],
        ]
    )
    gains = gains + core_swap(gains)
    return (
        output_vals,
        grad_inputs,
        raw_in * gain_one,
        conv_cols(2).T,
        out_gu,
        out_down,
        gains[0],
        gains[1],
        tap_grad,
    )


def solution(mesh):
    seq, cores = mesh.shape["seq"], mesh.shape["mp"]
    split = Mesh(np.asarray(mesh.devices).reshape(seq // 4, 2, 2, cores), ("z", "y", "x", "mp"))
    by = ("z", "y", "x")
    weights = (
        P(by, None, "mp"),
        P("mp", by),
        P(by, None, "mp"),
        P("mp", by),
        P(by),
        P(by),
        P(None, "mp", by),
    )
    return jax.shard_map(
        per_device,
        mesh=split,
        in_specs=(P(by, None), P(by)) + weights + (P(by, None),),
        out_specs=(P(by, None), P(by, None)) + weights,
        check_vma=False,
    )
```

```python
import functools

import jax
import jax.numpy as jnp
import numpy as np
from jax import lax
from jax.experimental import pallas as pl
from jax.experimental.pallas import tpu as pltpu
from jax.sharding import Mesh, PartitionSpec as P

epsilon = 1e-05
f32 = jnp.float32
bf16 = jnp.bfloat16
PLANE = ("y", "x")
SWAP = ((0, 1), (1, 0))
LANES = 128
VMEM_LIMIT = 50 * 1024 * 1024


def nn(left, right):
    return lax.dot_general(left, right, (((1,), (0,)), ((), ())), preferred_element_type=f32)


def nt(left, right):
    return lax.dot_general(left, right, (((1,), (1,)), ((), ())), preferred_element_type=f32)


def tn(left, right):
    return lax.dot_general(left, right, (((0,), (0,)), ((), ())), preferred_element_type=f32)


def after(value, *others):
    return lax.optimization_barrier((value,) + others)[0]


def together(*groups):
    flat = lax.optimization_barrier(tuple(value for group in groups for value in group))
    ends = np.cumsum([len(group) for group in groups])
    return [list(flat[end - len(group) : end]) for end, group in zip(ends, groups)]


def by_xor(stack, bits):
    places = np.arange(stack.shape[0])
    for level, bit in enumerate(bits):
        turned = jnp.stack([stack[int(p)] for p in places ^ (1 << level)])
        stack = jnp.where(bit, turned, stack)
    return stack


def plane_bits():
    return [lax.axis_index("x") == 1, lax.axis_index("y") == 1]


def plane_swap(value, offset):
    if offset == 1:
        return lax.ppermute(value, "x", SWAP)
    if offset == 2:
        return lax.ppermute(value, "y", SWAP)
    return lax.ppermute(value, PLANE, [(i, i ^ 3) for i in range(4)])


def core_swap(value):
    return lax.ppermute(value, "mp", SWAP)


def exchange_first(relative):
    return [relative[0]] + [plane_swap(relative[r], r) for r in (1, 2, 3)]


def exchange_second(got):
    return by_xor(jnp.stack(got), plane_bits())


def plane_exchange(stack):
    return exchange_second(exchange_first(by_xor(stack, plane_bits())))


def gather_first(top, low):
    return [plane_swap(part, offset) for offset in (1, 2) for part in (top, low)]


def gather_second(near):
    return [plane_swap(near[0], 2), plane_swap(near[3], 1)]


def plane_gather(own):
    half = own.shape[0] // 2
    near = gather_first(own[:half], own[half:])
    return [own] + near + gather_second(near)


def reduce_far(parts):
    return [plane_swap(parts[0], 1), plane_swap(parts[1], 2)]


def reduce_near(parts):
    return [plane_swap(parts[2], 1), plane_swap(parts[3], 2)]


def reduce_passed(parts, far):
    low_on = (parts[6].astype(f32) + far[0].astype(f32)).astype(bf16)
    top_on = (parts[5].astype(f32) + far[1].astype(f32)).astype(bf16)
    return [top_on, low_on], [plane_swap(top_on, 1), plane_swap(low_on, 2)]


def halo_forward(tails):
    planes = lax.axis_size("z")
    got = core_swap(tails)
    jump = [(2 * z + 1, 2 * z + 2) for z in range(planes - 1)]
    ordered = by_xor(jnp.moveaxis(tails, 1, 0), plane_bits())
    before = lax.ppermute(ordered[3], ("z", "mp"), jump)
    ordered = by_xor(jnp.moveaxis(got, 1, 0), plane_bits())
    shifted = by_xor(jnp.concatenate([before[None], ordered[:3]], axis=0), plane_bits())
    return jnp.where(lax.axis_index("mp") == 1, got, jnp.moveaxis(shifted, 0, 1))


def halo_backward(heads):
    planes = lax.axis_size("z")
    got = core_swap(heads)
    jump = [(2 * z + 2, 2 * z + 1) for z in range(planes - 1)]
    ordered = by_xor(jnp.moveaxis(heads, 1, 0), plane_bits())
    behind = lax.ppermute(ordered[0], ("z", "mp"), jump)
    ordered = by_xor(jnp.moveaxis(got, 1, 0), plane_bits())
    shifted = by_xor(jnp.concatenate([ordered[1:], behind[None]], axis=0), plane_bits())
    return jnp.where(lax.axis_index("mp") == 1, jnp.moveaxis(shifted, 0, 1), got)


def taps_turn(back):
    planes = lax.axis_size("z")
    pairs = [(s, (s % planes) * 4 + s // planes) for s in range(4 * planes)]
    return [(b, a) for a, b in pairs] if back else pairs


def call(body, out_shapes, *args, grid=None, in_specs=None, out_specs=None, prefetch=0, flops=0, aliases=None):
    def whole(value):
        zeros = (0,) * len(value.shape)
        return pl.BlockSpec(value.shape, lambda *_: zeros)

    if in_specs is None:
        in_specs = [whole(value) for value in args[prefetch:]]
    if out_specs is None:
        out_specs = [whole(value) for value in out_shapes]
    moved = sum(a.size * a.dtype.itemsize for a in args)
    moved += sum(o.size * o.dtype.itemsize for o in out_shapes)
    return pl.pallas_call(
        body,
        out_shape=out_shapes,
        grid_spec=pltpu.PrefetchScalarGridSpec(
            num_scalar_prefetch=prefetch,
            grid=grid or (1,),
            in_specs=in_specs,
            out_specs=out_specs,
        ),
        input_output_aliases=aliases or {},
        compiler_params=pltpu.CompilerParams(vmem_limit_bytes=VMEM_LIMIT),
        cost_estimate=pl.CostEstimate(flops=flops // 10000, bytes_accessed=moved // 10000, transcendentals=0),
    )(*args)


def out(shape, dtype):
    return jax.ShapeDtypeStruct(shape, dtype)


def spans(seg):
    half = seg // 2
    parts = [(0, 0, 0, seg)]
    for segment in (1, 2, 3):
        parts.append((2 * segment - 1, segment, 0, half))
        parts.append((2 * segment, segment, half, seg - half))
    return parts


BLOCKS = 7


def split_shapes(seg, width):
    half = seg // 2
    return [out((seg if place == 4 else half, width), bf16) for place in range(BLOCKS)]


def split_store(refs, segment, value):
    value = value.astype(bf16)
    half = value.shape[0] // 2
    if segment == 0:
        refs[4][...] = value
        return
    top, low = {1: (5, 2), 2: (3, 6), 3: (1, 0)}[segment]
    refs[top][...] = value[:half]
    refs[low][...] = value[half:]


def conv_project(hats, pack, seg, tap_len):
    planes, _, rows_taps, cols = pack.shape
    rows, chan = rows_taps - 16, cols // 4
    width = planes * rows

    def body(*refs):
        hat_refs, pack_ref = refs[:BLOCKS], refs[BLOCKS]
        b_ref, c_ref, x_ref, u_ref, keep_ref, taps_ref, tails_ref, gate_ref = refs[BLOCKS + 1 :]

        @pl.when(pl.program_id(0) == 0)
        def _():
            for segment, place in enumerate((0, 2, 4, 6)):
                below = hat_refs[place].shape[0] - 16
                begins = hat_refs[place][below:, :seg].astype(f32)[0:1]
                begins = jnp.transpose(jnp.broadcast_to(begins, (LANES, seg)))
                before = jnp.where(rows_of((seg, LANES)) == 0, 0.0, pltpu.roll(begins, 1, 0))
                keep_one = (1.0 - begins)[:, :1]
                keep_ref[0, segment] = keep_one
                keep_ref[1, segment] = ((1.0 - begins) * (1.0 - before))[:, :1]
                gate_ref[segment, 0:1] = keep_one[seg - 1 :]
                gate_ref[segment, 1:2] = jnp.ones((1, 1), f32)

        weights = pack_ref[:, 0, :rows, :].reshape(width, cols)
        for plane in range(planes):
            row = pack_ref[plane, 0, rows:, :].astype(f32)[0:1]
            for k in range(3):
                at = pl.ds(plane * tap_len, tap_len)
                taps_ref[0, k : k + 1, at] = row[:, k * tap_len : (k + 1) * tap_len]
        for place, segment, low, count in spans(seg):
            proj = nn(hat_refs[place][:count, :], weights)
            b_val, c_val, x_val = proj[:, :chan], proj[:, chan : 2 * chan], proj[:, 3 * chan :]
            at = (0, segment, pl.ds(low, count))
            b_ref[at] = b_val
            c_ref[at] = c_val
            x_ref[at] = x_val
            u_val = b_val * x_val
            u_ref[at] = u_val.astype(bf16)
            if low + count == seg:
                last = u_val[count - 2 :].astype(bf16).astype(f32) * gate_ref[segment]
                tails_ref[0, segment] = last.astype(bf16)

    shape = (2, 4, seg, chan)
    shapes = [out(shape, f32)] * 3 + [out(shape, bf16), out((2, 4, seg, 1), f32)]
    shapes += [out((2, 3, chan), f32), out((2, 4, 2, chan), bf16), out((4, 2, 1), f32)]

    def of_half(value):
        rest = value.shape[1:]
        return pl.BlockSpec((1,) + rest, lambda h: (h,) + (0,) * len(rest))

    def fixed(value):
        zeros = (0,) * len(value.shape)
        return pl.BlockSpec(value.shape, lambda h: zeros)

    results = call(
        body,
        shapes,
        *hats,
        pack,
        grid=(2,),
        in_specs=[fixed(v) for v in hats]
        + [pl.BlockSpec((planes, 1, rows_taps, cols), lambda h: (0, h, 0, 0))],
        out_specs=[of_half(v) for v in shapes[:4]]
        + [fixed(shapes[4]), of_half(shapes[5]), of_half(shapes[6]), fixed(shapes[7])],
        flops=2 * 4 * seg * width * cols * 2,
    )
    return results[:4], results[4:]


def by_segment(value):
    rest = value.shape[2:]
    return pl.BlockSpec((value.shape[0], 1) + rest, lambda s: (0, s) + (0,) * len(rest))


def every_step(value):
    zeros = (0,) * len(value.shape)
    return pl.BlockSpec(value.shape, lambda s: zeros)


def out_columns(pack):
    chan = pack.shape[3] // 4
    first, count = 2 * chan // LANES, -(-chan // LANES)
    block = pack.shape[:3] + (LANES,)
    return [
        pl.BlockSpec(block, functools.partial(lambda c, s: (0, 0, 0, c), first + k))
        for k in range(count)
    ]


def out_matrix(refs, half, rows, chan):
    parts = [ref[:, half, :rows, :].reshape(-1, LANES) for ref in refs]
    return jnp.concatenate(parts, axis=1)[:, :chan]


def rows_of(shape):
    return lax.broadcasted_iota(jnp.int32, shape, 0)


def earlier_rows(value, halo):
    row = rows_of(value.shape)
    one = jnp.where(row == 0, halo[1:2], pltpu.roll(value, 1, 0))
    two = jnp.where(row == 0, halo[0:1], jnp.where(row == 1, halo[1:2], pltpu.roll(value, 2, 0)))
    return one, two


def conv_mix(u_vals, halo, c_part, keeps, taps, pack, seg):
    planes, _, rows_taps, cols = pack.shape
    rows, chan = rows_taps - 16, cols // 4
    width = planes * rows

    columns = out_columns(pack)

    def body(u_ref, halo_ref, c_ref, keep_ref, taps_ref, *refs):
        pack_refs, (v_ref, y_ref, *split) = refs[: len(columns)], refs[len(columns) :]
        keep_one, keep_two = keep_ref[0, 0], keep_ref[1, 0]
        total = None
        for half in range(2):
            u_val = u_ref[half, 0].astype(f32)
            one, two = earlier_rows(u_val, halo_ref[half, 0])
            tap = taps_ref[half]
            v_val = tap[0:1] * u_val + tap[1:2] * keep_one * one + tap[2:3] * keep_two * two
            y_val = (c_ref[half, 0] * v_val).astype(bf16)
            v_ref[half, 0] = v_val
            y_ref[half, 0] = y_val
            term = nt(y_val, out_matrix(pack_refs, half, rows, chan))
            total = term if total is None else total + term
        for segment in range(4):

            @pl.when(pl.program_id(0) == segment)
            def _(segment=segment):
                split_store(split, segment, total)

    shape = (2, 4, seg, chan)
    shapes = [out(shape, f32), out(shape, bf16)] + split_shapes(seg, width)
    results = call(
        body,
        shapes,
        u_vals,
        halo,
        c_part,
        keeps,
        taps,
        *[pack] * len(columns),
        grid=(4,),
        in_specs=[by_segment(v) for v in (u_vals, halo, c_part, keeps)]
        + [every_step(taps)]
        + columns,
        out_specs=[by_segment(v) for v in shapes[:2]] + [every_step(v) for v in shapes[2:]],
        flops=2 * 4 * seg * width * 2 * chan,
    )
    return results[0], results[1], results[2:]


def conv_back(grad_mixer, u_vals, halo, c_part, v_vals, keeps, taps, pack, seg):
    planes, _, rows_taps, cols = pack.shape
    rows, chan = rows_taps - 16, cols // 4
    width = planes * rows

    columns = out_columns(pack)

    def body(*refs):
        mix_refs, refs = refs[:BLOCKS], refs[BLOCKS:]
        u_ref, halo_ref, c_ref, v_ref, keep_ref, taps_ref, *refs = refs
        pack_refs, refs = refs[: len(columns)], refs[len(columns) :]
        dc_ref, dv_ref, sums_ref, heads_ref = refs
        keep_one, keep_two = keep_ref[0, 0], keep_ref[1, 0]

        @pl.when(pl.program_id(0) == 0)
        def _():
            sums_ref[...] = jnp.zeros_like(sums_ref)

        for half in range(2):
            outs = out_matrix(pack_refs, half, rows, chan)
            for place, segment, low, count in spans(seg):

                @pl.when(pl.program_id(0) == segment)
                def _(place=place, low=low, count=count):
                    at = (half, 0, pl.ds(low, count))
                    grad_y = nn(mix_refs[place][:count, :], outs)
                    dc_ref[at] = (grad_y * v_ref[at]).astype(bf16)
                    dv_ref[at] = grad_y * c_ref[at]

            tap = taps_ref[half]
            u_val = u_ref[half, 0].astype(f32)
            one, two = earlier_rows(u_val, halo_ref[half, 0])
            grad_v = dv_ref[half, 0]
            once, twice = keep_one * grad_v, keep_two * grad_v
            for k, term in enumerate((grad_v * u_val, once * one, twice * two)):
                sums_ref[half, k : k + 1] += jnp.sum(term, axis=0, keepdims=True)
            heads_ref[half, 0, 0:1] = tap[2:3] * twice[0:1]
            heads_ref[half, 0, 1:2] = tap[1:2] * once[0:1] + tap[2:3] * twice[1:2]

    shape = (2, 4, seg, chan)
    shapes = [out(shape, bf16), out(shape, f32)]
    shapes += [out((2, 3, chan), f32), out((2, 4, 2, chan), f32)]
    return call(
        body,
        shapes,
        *grad_mixer,
        u_vals,
        halo,
        c_part,
        v_vals,
        keeps,
        taps,
        *[pack] * len(columns),
        grid=(4,),
        in_specs=[every_step(v) for v in grad_mixer]
        + [by_segment(v) for v in (u_vals, halo, c_part, v_vals, keeps)]
        + [every_step(taps)]
        + columns,
        out_specs=[by_segment(shapes[0]), by_segment(shapes[1])]
        + [every_step(shapes[2]), by_segment(shapes[3])],
        flops=2 * 4 * seg * width * 2 * chan,
    )


def conv_grads(grad_c, grad_v, back, b_part, x_part, keeps, taps, seg):
    chan = grad_v.shape[-1]

    def body(dc_ref, dv_ref, back_ref, b_ref, x_ref, keep_ref, taps_ref, dp_ref):
        row = rows_of((seg, chan))
        keep_one, keep_two = keep_ref[0, 0], keep_ref[1, 0]
        for half in range(2):
            tap = taps_ref[half]
            grad_val = dv_ref[half, 0]
            once = jnp.where(row == seg - 1, 0.0, pltpu.roll(keep_one * grad_val, seg - 1, 0))
            twice = jnp.where(row >= seg - 2, 0.0, pltpu.roll(keep_two * grad_val, seg - 2, 0))
            grad_u = tap[0:1] * grad_val + tap[1:2] * once + tap[2:3] * twice
            ends = back_ref[half, 0]
            grad_u = grad_u + jnp.where(
                row == seg - 2, ends[0:1], jnp.where(row == seg - 1, ends[1:2], 0.0)
            )
            grad_u = grad_u.astype(bf16).astype(f32)
            dp_ref[half] = jnp.concatenate(
                [
                    grad_u * x_ref[half, 0],
                    dc_ref[half, 0].astype(f32),
                    jnp.zeros((seg, chan), f32),
                    grad_u * b_ref[half, 0],
                ],
                axis=1,
            ).astype(bf16)

    return call(
        body,
        [out((2, 4 * seg, 4 * chan), bf16)],
        grad_c,
        grad_v,
        back,
        b_part,
        x_part,
        keeps,
        taps,
        grid=(4,),
        in_specs=[by_segment(v) for v in (grad_c, grad_v, back, b_part, x_part, keeps)]
        + [every_step(taps)],
        out_specs=[pl.BlockSpec((2, seg, 4 * chan), lambda s: (0, s, 0))],
    )[0]


def ffn_pack(gate, up, down, gain, place, cuts, chan_hid):
    rows = gate.shape[0]
    hid = chan_hid

    def body(place_ref, gate_ref, up_ref, down_ref, gain_ref, *outs):
        scale = gain_ref[...]
        for q in range(4):
            for (low, high), out_ref in zip(cuts, outs):
                tiles = high - low
                for t in range(tiles):
                    start = (low + t) * LANES
                    count = min(hid - start, LANES)
                    values = [
                        ref[:, q * hid + start : q * hid + start + count]
                        for ref in (gate_ref, up_ref, down_ref)
                    ]
                    values[0] = (values[0].astype(f32) * scale).astype(bf16)
                    values[1] = (values[1].astype(f32) * scale).astype(bf16)
                    if count < LANES:
                        fill = jnp.zeros((rows, LANES - count), bf16)
                        values = [jnp.concatenate([v, fill], axis=1) for v in values]
                    for value, column in zip(values, (2 * t, 2 * t + 1, 2 * tiles + t)):
                        out_ref[q ^ place_ref[0], :, column * LANES : (column + 1) * LANES] = value

    return call(
        body,
        [out((4, rows, 3 * LANES * (high - low)), bf16) for low, high in cuts],
        place,
        gate,
        up,
        down,
        gain,
        prefetch=1,
    )


def ffn_unpack(first, second, gate, up, gain, place, cuts, chan_hid):
    rows, half_f = gate.shape
    hid = chan_hid

    def body(place_ref, first_ref, second_ref, gate_ref, up_ref, gain_ref, gu_ref, down_ref, sum_ref):
        scale = gain_ref[...]
        total = jnp.zeros((rows, LANES), f32)
        for q in range(4):
            for (low, high), ref in zip(cuts, (first_ref, second_ref)):
                tiles = high - low
                for t in range(tiles):
                    start = (low + t) * LANES
                    count = min(hid - start, LANES)
                    at = q * hid + start
                    values = [
                        ref[q ^ place_ref[0], :, column * LANES : (column + 1) * LANES].astype(f32)
                        for column in (2 * t, 2 * t + 1, 2 * tiles + t)
                    ]
                    for side, w_ref in enumerate((gate_ref, up_ref)):
                        weight = w_ref[:, at : at + count].astype(f32)
                        if count < LANES:
                            fill = jnp.zeros((rows, LANES - count), f32)
                            weight = jnp.concatenate([weight, fill], axis=1)
                        total = total + values[side] * weight
                        gu_ref[:, side, at : at + count] = (values[side] * scale)[:, :count]
                    down_ref[:, at : at + count] = values[2][:, :count]
        sum_ref[...] = jnp.sum(total, axis=1, keepdims=True)

    return call(
        body,
        [out((rows, 2, half_f), f32), out((rows, half_f), f32), out((rows, 1), f32)],
        place,
        first,
        second,
        gate,
        up,
        gain,
        prefetch=1,
    )


def ffn_pass(hats, cots, pack, size, seg, segments, earlier=None):
    planes, _, rows, _ = pack.shape
    width = planes * rows
    tiles = size // LANES
    blocks = [span for span in spans(seg) if span[1] in segments]
    hats, cots = ([values[span[0]] for span in blocks] for values in (hats, cots))
    count_in = len(blocks)
    first = blocks[0][1]
    held_rows = len(segments) * seg

    def body(*refs):
        hat_refs, cot_refs = refs[:count_in], refs[count_in : 2 * count_in]
        gu_ref, down_ref = refs[2 * count_in : 2 * count_in + 2]
        a_ref, dg_ref = refs[-2:]
        downs = jnp.concatenate(
            [down_ref[:, half].reshape(width, LANES) for half in range(2)], axis=1
        )
        gus = [gu_ref[:, half].reshape(width, 2 * LANES) for half in range(2)]
        for hat_ref, cot_ref, (_, segment, low, count) in zip(hat_refs, cot_refs, blocks):
            at = pl.ds((segment - first) * seg + low, count)
            grad_act = nn(cot_ref[:count, :], downs)
            for half in range(2):
                vals = nn(hat_ref[:count, :], gus[half])
                gate, up = vals[:, :LANES], vals[:, LANES:]
                grad = grad_act[:, half * LANES : (half + 1) * LANES]
                sig = 1.0 / (1.0 + jnp.exp(-gate))
                silu = gate * sig
                a_ref[half, at, :] = (silu * up).astype(bf16)
                dg_ref[half, at, :LANES] = (grad * up * (sig + silu * (1.0 - sig))).astype(bf16)
                dg_ref[half, at, LANES:] = (grad * silu).astype(bf16)

    def held(value):
        return pl.BlockSpec(value.shape, lambda t: (0, 0))

    tokens = 4 * seg
    place = first * seg // held_rows
    args = [*hats, *cots, pack, pack]
    specs = [held(v) for v in (*hats, *cots)] + [
        pl.BlockSpec((planes, 2, rows, 2 * LANES), lambda t: (0, 0, 0, t)),
        pl.BlockSpec((planes, 2, rows, LANES), lambda t: (0, 0, 0, 2 * tiles + t)),
    ]
    aliases = None
    if earlier is not None:
        aliases = {len(args): 0, len(args) + 1: 1}
        args += list(earlier)
        specs += [pl.BlockSpec(memory_space=pl.ANY)] * 2
    return call(
        body,
        [out((2, tokens, size), bf16), out((2, tokens, 2 * size), bf16)],
        *args,
        grid=(tiles,),
        in_specs=specs,
        out_specs=[
            pl.BlockSpec((2, held_rows, LANES), lambda t: (0, place, t)),
            pl.BlockSpec((2, held_rows, 2 * LANES), lambda t: (0, place, t)),
        ],
        flops=2 * held_rows * width * 6 * size,
        aliases=aliases,
    )


def turned_back(lefts, packs, place, rows, seg):
    planes = packs[0].shape[0]
    width = planes * rows
    group = max(1, 2 * planes // 4)
    wide = group * rows

    def body(*refs):
        count = len(lefts)
        left_refs, pack_refs, split = refs[:count], refs[count : 2 * count], refs[2 * count :]
        weights = [
            [ref[:, half].reshape(wide, ref.shape[-1]) for half in range(2)] for ref in pack_refs
        ]
        for segment in range(4):
            total = None
            for left_ref, pair in zip(left_refs, weights):
                for half in range(2):
                    term = nt(left_ref[half, segment * seg : (segment + 1) * seg, :], pair[half])
                    total = term if total is None else total + term
            split_store(split, segment, total)

    cols = [left.shape[-1] for left in lefts]
    shapes = split_shapes(seg, width)
    return call(
        body,
        shapes,
        *lefts,
        *packs,
        grid=(planes // group,),
        in_specs=[pl.BlockSpec(left.shape, lambda i: (0, 0, 0)) for left in lefts]
        + [
            pl.BlockSpec((group, 2, rows, c), functools.partial(lambda p, i: (i, 0, 0, p), place))
            for c in cols
        ],
        out_specs=[pl.BlockSpec((shape.shape[0], wide), lambda i: (0, i)) for shape in shapes],
        flops=2 * 4 * seg * width * 2 * sum(cols),
    )


def weight_grad(lefts, right, others, other_right, at, rows, seg, extra=None):
    width = lefts[0].shape[1]
    wide = 384
    group = wide // rows
    first, second = right.shape[-1], other_right.shape[-1]
    cols = max(first, at + second)
    below = 0 if extra is None else extra.shape[2]

    def body(*refs):
        left_refs, other_refs, refs = refs[:BLOCKS], refs[BLOCKS : 2 * BLOCKS], refs[2 * BLOCKS :]
        right_ref, other_ref, out_ref = refs[0], refs[1], refs[-1]

        def gathered(places):
            return jnp.concatenate(
                [places[place][:count, :] for place, _, _, count in spans(seg)], axis=0
            )

        def put(low, value):
            value = value.astype(bf16).reshape(group, rows, value.shape[-1])
            out_ref[:, 0, :rows, low : low + value.shape[-1]] = value

        put(0, tn(gathered(left_refs), right_ref[0]))
        put(at, tn(gathered(other_refs), other_ref[0]))
        if extra is not None:
            out_ref[:, 0, rows:, :] = refs[2][:, 0]

    def column(value):
        return pl.BlockSpec((value.shape[0], wide), lambda h, i: (0, i))

    def chosen(value):
        return pl.BlockSpec((1,) + value.shape[1:], lambda h, i: (h, 0, 0))

    args = [*lefts, *others, right, other_right]
    specs = [column(v) for v in (*lefts, *others)] + [chosen(right), chosen(other_right)]
    if extra is not None:
        args.append(extra)
        specs.append(pl.BlockSpec((group, 1, below, cols), lambda h, i: (i, h, 0, 0)))
    return call(
        body,
        [out((width // rows, 2, rows + below, cols), bf16)],
        *args,
        grid=(2, width // wide),
        in_specs=specs,
        out_specs=[
            pl.BlockSpec((group, 1, rows + below, cols), lambda h, i: (i, h, 0, 0)),
        ],
        flops=2 * 4 * seg * width * cols * 2,
    )[0]


def sum_parts(own_ref, last_refs):
    top_passed, low_passed, low_near, top_near = [ref[...].astype(f32) for ref in last_refs]
    half = top_near.shape[0]
    own = own_ref[...].astype(f32)
    return jnp.concatenate(
        [own[:half] + top_near + top_passed, own[half:] + low_near + low_passed], axis=0
    )


def halves(shape, dtype):
    return [out((shape[0] // 2,) + shape[1:], dtype)] * 2


def store_halves(value, refs):
    half = value.shape[0] // 2
    refs[0][...] = value[:half]
    refs[1][...] = value[half:]


def middle_norm(parts, last, tokens, core):
    rows, width = parts[4].shape

    def body(core_ref, own_ref, *refs):
        last_refs, token_ref, mid_ref, inv_ref, hat_ref, *half_refs = refs[:4], *refs[4:]
        middle = token_ref[...].astype(f32) + sum_parts(own_ref, last_refs)
        inv = lax.rsqrt(jnp.mean(middle * middle, axis=-1, keepdims=True) + epsilon)
        hat = (middle * inv).astype(bf16)
        mid_ref[...] = middle
        inv_ref[...] = inv
        hat_ref[...] = hat
        store_halves(hat, half_refs)

    shape = (rows, width)
    return on_core(
        body,
        [out(shape, f32), out((rows, 1), f32), out(shape, bf16)] + halves(shape, bf16),
        core,
        [parts[4], *last],
        [tokens],
    )


def middle_back(parts, last, middle, inv, cot, core):
    rows, width = parts[4].shape

    def body(core_ref, own_ref, *refs):
        last_refs, mid_ref, inv_ref, cot_ref, grad_ref, round_ref, *half_refs = (
            refs[:4],
            *refs[4:],
        )
        grad = sum_parts(own_ref, last_refs)
        inv = inv_ref[...]
        hat = mid_ref[...] * inv
        inner = jnp.mean(grad * hat, axis=-1, keepdims=True)
        grad = cot_ref[...].astype(f32) + inv * (grad - hat * inner)
        grad_ref[...] = grad
        rounded = grad.astype(bf16)
        round_ref[...] = rounded
        store_halves(rounded, half_refs)

    shape = (rows, width)
    return on_core(
        body,
        [out(shape, f32), out(shape, bf16)] + halves(shape, bf16),
        core,
        [parts[4], *last, middle, inv, cot],
        [],
    )


def on_core(body, shapes, core, args, by_core, both=()):
    def whole(value):
        zeros = (0,) * len(value.shape)
        return pl.BlockSpec(value.shape, lambda i, c: zeros)

    def part(value):
        return pl.BlockSpec((value.shape[0] // 2, value.shape[1]), lambda i, c: (c[0], 0))

    return call(
        body,
        list(shapes) + list(both),
        core,
        *args,
        *by_core,
        in_specs=[whole(v) for v in args] + [part(v) for v in by_core],
        out_specs=[whole(v) for v in shapes] + [part(v) for v in both],
        prefetch=1,
    )


def block_out(parts, last, middle, core):
    rows, width = middle.shape

    def body(core_ref, own_ref, *refs):
        last_refs, mid_ref, result_ref, both_ref = refs[:4], *refs[4:]
        result = (mid_ref[...] + sum_parts(own_ref, last_refs)).astype(bf16)
        result_ref[...] = result
        both_ref[...] = result

    return on_core(
        body,
        [out((rows, width), bf16)],
        core,
        [parts[4], *last, middle],
        [],
        [out((2 * rows, width), bf16)],
    )


def tokens_back(parts, last, grad_middle, tokens, core):
    rows, width = grad_middle.shape

    def body(core_ref, own_ref, *refs):
        last_refs, grad_ref, token_ref, result_ref, both_ref = refs[:4], *refs[4:]
        grad = sum_parts(own_ref, last_refs)
        values = token_ref[...].astype(f32)
        inv = lax.rsqrt(jnp.mean(values * values, axis=-1, keepdims=True) + epsilon)
        hat = values * inv
        inner = jnp.mean(grad * hat, axis=-1, keepdims=True)
        result = grad_ref[...] + inv * (grad - hat * inner)
        result_ref[...] = result
        both_ref[...] = result

    return on_core(
        body,
        [out((rows, width), f32)],
        core,
        [parts[4], *last, grad_middle],
        [tokens],
        [out((2 * rows, width), f32)],
    )


def fill_other(both, other, core):
    rows, width = other.shape

    def body(core_ref, other_ref, _, both_ref):
        both_ref[...] = other_ref[...]

    return call(
        body,
        [out(both.shape, both.dtype)],
        core,
        other,
        both,
        in_specs=[
            pl.BlockSpec((rows, width), lambda i, c: (0, 0)),
            pl.BlockSpec(memory_space=pl.ANY),
        ],
        out_specs=[pl.BlockSpec((rows, width), lambda i, c: (1 - c[0], 0))],
        prefetch=1,
        aliases={2: 0},
    )[0]


def per_device(
    tokens, starts, w_in, w_out, gate_up, w_down, gain_mix, gain_ffn, conv_taps, cotangent
):
    core = lax.axis_index("mp")
    planes = lax.axis_size("z")
    rows, _, half_c = w_in.shape
    half_f = w_down.shape[0]
    width = tokens.shape[1]
    seg = tokens.shape[0] // 2
    chan, hid = half_c // 4, half_f // 4
    plane_rows = 4 * rows
    tap_len = conv_taps.shape[2]
    tiles = -(-hid // LANES)
    cuts = ((0, tiles // 2 + 1), (tiles // 2 + 1, tiles))
    sizes = [LANES * (high - low) for low, high in cuts]
    own_half = core.astype(jnp.int32).reshape(1)

    def mine(value):
        return lax.dynamic_slice_in_dim(value, core * seg, seg, axis=0)

    gain_one = gain_mix.astype(f32)[:, None, None]
    gain_two = gain_ffn.astype(f32)[:, None, None]
    in_scaled = (w_in.astype(f32) * gain_one).astype(bf16)
    out_turned = w_out.T

    def conv_columns(q):
        at = slice(q * chan, (q + 1) * chan)
        return [in_scaled[:, 0, at], in_scaled[:, 1, at], out_turned[:, at], in_scaled[:, 2, at]]

    conv_quart = jnp.stack([jnp.concatenate(conv_columns(q), axis=1) for q in range(4)])
    conv_quart = by_xor(conv_quart, plane_bits())
    tap_piece = lax.ppermute(conv_taps.reshape(1, -1), ("z",) + PLANE, taps_turn(False))
    tap_rows = jnp.pad(tap_piece, ((0, 15), (0, 4 * chan - 3 * tap_len)))
    conv_got = exchange_first(conv_quart)

    def over_all(value):
        value = lax.all_gather(value, ("z", "mp"), axis=0, tiled=False)
        return value.reshape((planes, 2) + value.shape[1:])

    inputs = mine(tokens).astype(f32)
    inv_mix = lax.rsqrt(jnp.mean(inputs * inputs, axis=-1, keepdims=True) + epsilon)
    hat_mix = inputs * inv_mix
    hat_own = hat_mix.astype(bf16)
    begin_rows = jnp.pad(mine(starts).astype(bf16)[None], ((0, 15), (0, width - seg)))
    half_seg = seg // 2
    hat_low = jnp.concatenate([hat_own[half_seg:], begin_rows], axis=0)
    hat_top = hat_own[:half_seg]
    hat_own = jnp.concatenate([hat_own, begin_rows], axis=0)
    hat_own, hat_top, hat_low = lax.optimization_barrier((hat_own, hat_top, hat_low, conv_quart))[:3]
    hats_near = gather_first(hat_top, hat_low)
    conv_pack = exchange_second(after(conv_got, hat_own)).reshape(plane_rows, 4 * chan)
    conv_pack = jnp.concatenate([conv_pack, tap_rows], axis=0)
    conv_all = over_all(conv_pack)
    cot = mine(cotangent)

    place = (2 * lax.axis_index("y") + lax.axis_index("x")).astype(jnp.int32).reshape(1)
    packs = ffn_pack(
        gate_up[:, 0], gate_up[:, 1], w_down.T, gain_two[:, 0], place, cuts, hid
    )
    first_quart, second_quart = packs
    hats_near, (first_quart,) = together(hats_near, (first_quart,))
    hats = [hat_own] + hats_near + gather_second(hats_near)
    first_got = exchange_first(after(first_quart, *hats[5:]))
    cot, cot_top, cot_low = lax.optimization_barrier(
        (cot, cot[:half_seg], cot[half_seg:], *hats[5:])
    )[:3]
    cots_near = gather_first(cot_top, cot_low)

    projected, marks = conv_project(hats, conv_all, seg, tap_len)
    projected, marks, (second_quart,), first_got = together(
        projected, marks, (second_quart,), first_got
    )
    first_pack = exchange_second(first_got).reshape(plane_rows, -1)
    b_part, c_part, x_part, mixed_in = projected
    keeps, taps, tails, tail_gate = marks
    second_got = exchange_first(second_quart)
    halo = halo_forward(tails).astype(f32)
    convolved, gated, mixer = conv_mix(mixed_in, halo, c_part, keeps, taps, conv_all, seg)
    mixer, second_got, cots_near = together(mixer, second_got, cots_near)
    far, near = reduce_far(mixer), reduce_near(mixer)
    second_pack = exchange_second(second_got).reshape(plane_rows, -1)
    ffn_all = [over_all(first_pack), over_all(second_pack)]
    far, near, mixer, _ = together(far, near, mixer, (second_pack,))
    passed = reduce_passed(mixer, far)[1]
    last, mixer = together(passed + near, mixer)
    middle, inv_ffn, hat_own, hat_top, hat_low = middle_norm(mixer, last, tokens, own_half)

    near = gather_first(hat_top, hat_low)

    def first_cut(segment, earlier):
        return ffn_pass(hats_two, cots, ffn_all[0], sizes[0], seg, (segment,), earlier)

    hats_two, cots = [hat_own], [cot] + cots_near
    done_one = first_cut(0, None)
    done_one, near, cots_near = together(done_one, near, cots_near)
    hats_two, cots = [hat_own] + near, [cot] + cots_near
    far, cots_far = gather_second(near), gather_second(cots_near)
    done_one = first_cut(2, first_cut(1, done_one))
    done_one, far, cots_far = together(done_one, far, cots_far)
    hats_two, cots = hats_two + far, cots + cots_far

    def ordered(value):
        stack = by_xor(value.reshape(4, rows, -1), plane_bits())
        return [stack[r] for r in range(4)]

    def over_owners(value):
        value = value.reshape((2 * planes,) + value.shape[2:])
        return lax.psum_scatter(value, ("z", "mp"), scatter_dimension=0, tiled=False)

    acts_one, grads_one = first_cut(3, done_one)
    sum_one = weight_grad(hats_two, grads_one, cots, acts_one, 2 * sizes[0], plane_rows, seg)
    red_one = over_owners(sum_one)
    second_all = after(ffn_all[1], sum_one)
    acts_two, grads_two = ffn_pass(hats_two, cots, second_all, sizes[1], seg, (0, 1, 2, 3))
    grad_hat2 = turned_back([grads_one, grads_two], [ffn_all[0], second_all], 0, plane_rows, seg)
    far, near = reduce_far(grad_hat2), reduce_near(grad_hat2)
    acts_two, grads_two = lax.optimization_barrier((acts_two, grads_two, *grad_hat2))[:2]
    sum_two = weight_grad(hats_two, grads_two, cots, acts_two, 2 * sizes[1], plane_rows, seg)
    far, near, grad_hat2, (sum_two,) = together(far, near, grad_hat2, (sum_two,))
    red_two = over_owners(sum_two)
    sent, passed = reduce_passed(grad_hat2, far)
    acts_last = lax.optimization_barrier((acts_two, *sent))[0]
    ffn_out = turned_back([acts_one, acts_last], [ffn_all[0], second_all], 2, plane_rows, seg)
    last, ffn_out, grad_hat2 = together(passed + near, ffn_out, grad_hat2)
    grad_middle, mix_own, mix_top, mix_low = middle_back(
        grad_hat2, last, middle, inv_ffn, cot, own_half
    )

    near = gather_first(mix_top, mix_low)
    near, (back_one,) = together(near, (red_one,))
    grad_mixer = [mix_own] + near + gather_second(near)
    ffn_out, grad_mixer, back_one = together(ffn_out, grad_mixer, ordered(back_one))
    ffn_far = reduce_far(ffn_out)
    grad_c, grad_v, tap_sums, heads = conv_back(
        grad_mixer, mixed_in, halo, c_part, convolved, keeps, taps, conv_all, seg
    )
    (heads,), ffn_far, ffn_out = together((heads,), ffn_far, ffn_out)
    ffn_passed = reduce_passed(ffn_out, ffn_far)[1]
    back = halo_backward(heads) * tail_gate
    grad_proj = conv_grads(grad_c, grad_v, back, b_part, x_part, keeps, taps, seg)
    (grad_proj,), ffn_passed, back_one = together((grad_proj,), ffn_passed, back_one)
    gated = gated.reshape(2, 4 * seg, chan)
    tap_rows = jnp.transpose(tap_sums.reshape(2, 3, planes, tap_len), (2, 0, 1, 3))
    tap_rows = tap_rows.reshape(planes, 2, 1, 3 * tap_len).astype(bf16)
    tap_rows = jnp.pad(tap_rows, ((0, 0), (0, 0), (0, 15), (0, 4 * chan - 3 * tap_len)))
    sum_conv = weight_grad(
        hats, grad_proj, grad_mixer, gated, 2 * chan, plane_rows, seg, tap_rows
    )
    first_got = exchange_first(back_one)
    (sum_held,), first_got = together((sum_conv,), first_got)
    red_conv = over_owners(sum_held)
    ffn_near = reduce_near(ffn_out)
    grad_hat1 = turned_back([after(grad_proj, sum_conv)], [conv_all], 0, plane_rows, seg)
    grad_hat1, ffn_near, ffn_out, (middle, back_two) = together(
        grad_hat1, ffn_near, ffn_out, (middle, red_two)
    )
    far, near = reduce_far(grad_hat1), reduce_near(grad_hat1)
    back_two = ordered(back_two)
    far, near, grad_hat1, back_two, first_got, ffn_out, ffn_near, (middle,) = together(
        far, near, grad_hat1, back_two, first_got, ffn_out, ffn_near, (middle,)
    )
    passed = reduce_passed(grad_hat1, far)[1]
    second_got = exchange_first(back_two)
    out_own, out_both = block_out(ffn_out, ffn_passed + ffn_near, middle, own_half)

    conv_got = exchange_first(ordered(red_conv[:plane_rows]))
    passed, near, grad_hat1, second_got, conv_got, (out_own, out_both) = together(
        passed, near, grad_hat1, second_got, conv_got, (out_own, out_both)
    )
    output_vals = fill_other(out_both, core_swap(out_own), own_half)
    grad_own, grad_both = tokens_back(grad_hat1, passed + near, grad_middle, tokens, own_half)
    second_got, _ = together(second_got, (grad_own,))
    grad_inputs = fill_other(grad_both, core_swap(grad_own), own_half)
    out_gu, down_turned, gain_sum = ffn_unpack(
        jnp.stack(first_got),
        jnp.stack(second_got),
        gate_up[:, 0],
        gate_up[:, 1],
        gain_two[:, 0],
        place,
        cuts,
        hid,
    )
    out_down = down_turned.T
    conv_grad = exchange_second(conv_got).astype(f32)
    tap_grad = lax.ppermute(
        red_conv[plane_rows, : 3 * tap_len].astype(f32).reshape(3, 1, tap_len),
        ("z",) + PLANE,
        taps_turn(True),
    )

    def conv_cols(k):
        return jnp.concatenate(
            [conv_grad[q, :, k * chan : (k + 1) * chan] for q in range(4)], axis=1
        )

    raw_in = jnp.stack([conv_cols(k) for k in (0, 1, 3)], axis=1)
    gains = jnp.stack(
        [
            jnp.sum(raw_in * w_in.astype(f32), axis=(1, 2)),
            gain_sum[:, 0],
        ]
    )
    gains = gains + core_swap(gains)
    return (
        output_vals,
        grad_inputs,
        raw_in * gain_one,
        conv_cols(2).T,
        out_gu,
        out_down,
        gains[0],
        gains[1],
        tap_grad,
    )


def solution(mesh):
    seq, cores = mesh.shape["seq"], mesh.shape["mp"]
    split = Mesh(np.asarray(mesh.devices).reshape(seq // 4, 2, 2, cores), ("z", "y", "x", "mp"))
    by = ("z", "y", "x")
    weights = (
        P(by, None, "mp"),
        P("mp", by),
        P(by, None, "mp"),
        P("mp", by),
        P(by),
        P(by),
        P(None, "mp", by),
    )
    return jax.shard_map(
        per_device,
        mesh=split,
        in_specs=(P(by, None), P(by)) + weights + (P(by, None),),
        out_specs=(P(by, None), P(by, None)) + weights,
        check_vma=False,
    )
```
